256 devices in a mesh: dp: 16 (over z, core), expert: 16 (over x, y).
Axes of the slice: x: 4, y: 4, z: 8, core: 2. Of those that a mesh axis runs over, the one named last changes fastest.
Arguments:
- tokens: bfloat16 [32768, 2048], P(('dp', 'expert')), may hold values from -6 to 6
- cotangent: bfloat16 [32768, 2048], P(('dp', 'expert')), may hold values from -1.5 to 1.5
- picks: int32 [16, 16, 256], P('dp'), may hold values from 0 to 2047, as said below
- gates: float32 [16, 16, 256], P('dp', 'expert'), may hold values from 0.25 to 1
- w_gate: bfloat16 [16, 2048, 768], P('expert'), may hold values from -0.125 to 0.125
- w_up: bfloat16 [16, 2048, 768], P('expert'), may hold values from -0.125 to 0.125
- w_down: bfloat16 [16, 768, 2048], P('expert'), may hold values from -0.21875 to 0.21875
Outputs:
- token_grads: bfloat16 [32768, 2048], P(('dp', 'expert'))
- gate_grads: float32 [16, 16, 256], P('dp', 'expert')
- grad_gate: bfloat16 [16, 2048, 768], P('expert', 'dp')
- grad_up: bfloat16 [16, 2048, 768], P('expert', 'dp')
- grad_down: bfloat16 [16, 768, 2048], P('expert', None, 'dp')
The draws below stay inside these ranges and needn't reach their ends.
Inputs may be any that keep to these rules, and one draw needn't show every extreme that they name: Entry [g, e, c] is a token index within group g; token j * 128 + t of a group is local row t of device j along expert. An expert's 256 picks in a group are distinct and ascending. At most 24 of them lie among one device's tokens, and for every group and expert exactly 24 lie among some device's tokens.
All inputs are finite; a program needn't handle non-finite values.
Results may differ from the reference program's by a relative error of at most 0.023.
Values may be sent and summed in bfloat16 or wider, within the bound.
No kernel may reach another device: no remote copies, remote signals or barrier semaphores. Data moves between devices by JAX's collectives and lax.ppermute only.
A program may use at most 128 MiB of HBM per device.

```python
import jax
import jax.numpy as jnp
from jax import lax

D = 2048
FF = 768
TOK_DEV = 128
EXPERTS = 16
CAP = 256
MOST = 24
TOKENS = 32768
N_DP = 16
N_EXPERT = 16


def expert_picks(one_key):
    key_hot, key_bias, key_noise, key_tokens = jax.random.split(one_key, 4)
    hot_source = jax.random.randint(key_hot, (), 0, N_EXPERT)
    source_bias = jax.random.randint(key_bias, (N_EXPERT,), 0, 3)
    noise = jax.random.randint(key_noise, (N_EXPERT, MOST), 0, 8192)
    flat_ids = jnp.arange(N_EXPERT * MOST, dtype=jnp.int32).reshape(N_EXPERT, MOST)
    score = (source_bias[:, None] * 4096 + noise) * (N_EXPERT * MOST) + flat_ids
    pool_source = jnp.arange(N_EXPERT, dtype=jnp.int32)[:, None] + jnp.zeros((N_EXPERT, MOST), jnp.int32)
    score = jnp.where(pool_source == hot_source, -1, score).reshape(-1)
    ranked = jnp.argsort(-score)
    chosen = jnp.zeros((N_EXPERT * MOST,), jnp.int32).at[ranked[:CAP - MOST]].set(1)
    counts = jnp.sum(chosen.reshape(N_EXPERT, MOST), axis=1)
    counts = counts.at[hot_source].set(MOST)
    token_noise = jax.random.randint(key_tokens, (N_EXPERT, TOK_DEV), 0, 2 ** 20)
    token_score = token_noise * TOK_DEV + jnp.arange(TOK_DEV, dtype=jnp.int32)[None, :]
    token_rank = jnp.argsort(jnp.argsort(token_score, axis=1), axis=1)
    taken = token_rank < counts[:, None]
    global_ids = jnp.arange(N_EXPERT * TOK_DEV, dtype=jnp.int32).reshape(N_EXPERT, TOK_DEV)
    sort_keys = jnp.where(taken, 0, 1) * (N_EXPERT * TOK_DEV) + global_ids
    return jnp.sort(sort_keys.reshape(-1))[:CAP]


def draw_picks(key, part):
    key = jax.random.fold_in(key, 11)
    expert_keys = jax.random.split(key, N_DP * EXPERTS)
    return jax.vmap(expert_picks)(expert_keys).reshape(N_DP, EXPERTS, CAP).astype(jnp.int32)


def block_scale(own_key, extent, cuts, least, largest):
    gain, own = 1.0, jax.random.fold_in(own_key, 6)
    for position, parts in cuts:
        draws = jnp.exp(jax.random.uniform(jax.random.fold_in(own, position), (parts,), jnp.float32, least / len(cuts), largest / len(cuts)))
        gain = gain * jnp.repeat(draws, extent[position] // parts).reshape([-1 if axis == position else 1 for axis in range(len(extent))])
    return gain


def normal_values(stream_key, dims, width, limit, pieces=(), held_as=jnp.bfloat16):
    gain = block_scale(stream_key, dims, pieces, -0.22, 0.18) if pieces else 1.0
    result = jax.random.normal(stream_key, dims, jnp.float32) * width * gain
    return jnp.minimum(jnp.maximum(result, -limit), limit).astype(held_as)


def setup_inputs(seed: int = 0) -> dict:
    key_list = jax.random.split(jax.random.key(seed), 8)
    tokens = normal_values(key_list[0], (TOKENS, D), 1.0, 6.0, ((0, 256),))
    cotangent = normal_values(key_list[1], (TOKENS, D), 0.25, 1.5, ((0, 256),))
    picks = draw_picks(jax.random.fold_in(key_list[7], 71), 0)
    gates = jnp.clip(0.25 + 0.75 * jax.random.uniform(key_list[3], (N_DP, EXPERTS, CAP), jnp.float32) ** block_scale(key_list[3], (N_DP, EXPERTS, CAP), ((0, 16), (1, 16)), -0.2, 0.2), 0.25, 1.0)
    w_gate = normal_values(key_list[4], (EXPERTS, D, FF), D ** -0.5, 0.125, ((0, 16),))
    w_up = normal_values(key_list[5], (EXPERTS, D, FF), D ** -0.5, 0.125, ((0, 16),))
    w_down = normal_values(key_list[6], (EXPERTS, FF, D), FF ** -0.5, 0.21875, ((0, 16),))
    return dict(tokens=tokens, cotangent=cotangent, picks=picks, gates=gates, w_gate=w_gate, w_up=w_up, w_down=w_down)


def expert_backward(expert_rows, grad_rows, gate_rows, gate_weight, up_weight, down_weight):
    gate_pre = jnp.dot(expert_rows, gate_weight, preferred_element_type=jnp.float32)
    up_pre = jnp.dot(expert_rows, up_weight, preferred_element_type=jnp.float32)
    sigmoid_gate = jax.nn.sigmoid(gate_pre)
    activated = gate_pre * sigmoid_gate
    hidden = (activated * up_pre).astype(jnp.bfloat16)
    output = jnp.dot(hidden, down_weight, preferred_element_type=jnp.float32)
    grad_float = grad_rows.astype(jnp.float32)
    slot_grads = jnp.sum(grad_float * output, axis=1)
    scaled_grad = (gate_rows[:, None] * grad_float).astype(jnp.bfloat16)
    hidden_grad = jnp.dot(scaled_grad, down_weight.T, preferred_element_type=jnp.float32)
    gate_pre_grad = (hidden_grad * up_pre * sigmoid_gate * (1.0 + gate_pre * (1.0 - sigmoid_gate))).astype(jnp.bfloat16)
    up_pre_grad = (hidden_grad * activated).astype(jnp.bfloat16)
    row_grads = (jnp.dot(gate_pre_grad, gate_weight.T, preferred_element_type=jnp.float32)
                 + jnp.dot(up_pre_grad, up_weight.T, preferred_element_type=jnp.float32)).astype(jnp.bfloat16)
    return slot_grads, row_grads, hidden, scaled_grad, gate_pre_grad, up_pre_grad


def reference(tokens, cotangent, picks, gates, w_gate, w_up, w_down):
    group_rows = N_EXPERT * TOK_DEV
    token_groups = tokens.reshape(N_DP, group_rows, D)
    grad_groups = cotangent.reshape(N_DP, group_rows, D)

    def one_group(totals, inputs):
        group_tokens, group_grads, pick_table, gate_table = inputs

        def one_expert(summed, item):
            pick_row, gate_row, gate_weight, up_weight, down_weight = item
            expert_rows = jnp.take(group_tokens, pick_row, axis=0)
            grad_rows = jnp.take(group_grads, pick_row, axis=0)
            slot_grads, row_grads, hidden, scaled_grad, gate_pre_grad, up_pre_grad = expert_backward(
                expert_rows, grad_rows, gate_row, gate_weight, up_weight, down_weight)
            summed = summed.at[pick_row].add(row_grads.astype(jnp.float32))
            part_gate = jnp.dot(expert_rows.T, gate_pre_grad, preferred_element_type=jnp.float32).astype(jnp.bfloat16)
            part_up = jnp.dot(expert_rows.T, up_pre_grad, preferred_element_type=jnp.float32).astype(jnp.bfloat16)
            part_down = jnp.dot(hidden.T, scaled_grad, preferred_element_type=jnp.float32).astype(jnp.bfloat16)
            return summed, (slot_grads, part_gate, part_up, part_down)

        start_sum = jnp.zeros((group_rows, D), jnp.float32)
        summed, (slot_grads, part_gate, part_up, part_down) = lax.scan(
            one_expert, start_sum, (pick_table, gate_table, w_gate, w_up, w_down))
        totals = (totals[0] + part_gate.astype(jnp.float32), totals[1] + part_up.astype(jnp.float32),
                  totals[2] + part_down.astype(jnp.float32))
        return totals, (summed.astype(jnp.bfloat16), slot_grads)

    start_totals = (jnp.zeros((EXPERTS, D, FF), jnp.float32), jnp.zeros((EXPERTS, D, FF), jnp.float32),
                    jnp.zeros((EXPERTS, FF, D), jnp.float32))
    totals, (token_grads, gate_grads) = lax.scan(one_group, start_totals, (token_groups, grad_groups, picks, gates))
    return (token_grads.reshape(TOKENS, D), gate_grads, totals[0].astype(jnp.bfloat16),
            totals[1].astype(jnp.bfloat16), totals[2].astype(jnp.bfloat16))
```

```python
import jax
import jax.numpy as jnp
from jax import lax
from jax.sharding import PartitionSpec as P

BF16 = jnp.bfloat16
F32 = jnp.float32


def dot_nn(left, right):
    return jnp.dot(left, right, preferred_element_type=F32)


def dot_nt(left, right):
    return lax.dot_general(left, right, (((1,), (1,)), ((), ())), preferred_element_type=F32)


def dot_tn(left, right):
    return lax.dot_general(left, right, (((0,), (0,)), ((), ())), preferred_element_type=F32)


def swap_cores(array):
    size = lax.axis_size("dp")
    return lax.ppermute(array, "dp", [(i, i ^ 1) for i in range(size)])


def next_chip(array, sign):
    size = lax.axis_size("dp")
    return lax.ppermute(array, "dp", [(i, (i + 2 * sign) % size) for i in range(size)])


def chain(chunk_of, steps, sign):
    if steps == 0:
        return None
    total = chunk_of(sign * steps)
    for distance in range(steps - 1, -1, -1):
        got = next_chip(total, sign)
        if distance:
            total = (got.astype(F32) + chunk_of(sign * distance).astype(F32)).astype(BF16)
    return got


def reduce_chunks(chunk_of, far_side, chips):
    far = chips // 2
    near = chips - 1 - far
    first = chain(chunk_of, far, far_side)
    second = chain(chunk_of, near, -far_side)
    total = chunk_of(0).astype(F32)
    for part in (first, second):
        if part is not None:
            total = total + part.astype(F32)
    return total.astype(BF16)


def body(tokens, cotangent, picks, gates, w_gate, w_up, w_down):
    node_count = lax.axis_size("expert")
    self_index = lax.axis_index("expert")
    dp_size = lax.axis_size("dp")
    dp_index = lax.axis_index("dp").astype(jnp.uint32)
    chips = dp_size // 2
    core = dp_index & 1
    chip = dp_index >> 1
    tok_dev, width = tokens.shape
    slot_count = gates.shape[2]
    most = max(2, 3 * slot_count // (2 * node_count))
    hidden_width = w_gate.shape[2]
    block = width // dp_size

    table = picks[0]
    local = table - self_index * tok_dev
    token_range = jnp.arange(tok_dev, dtype=jnp.int32)
    member = jnp.any(local[:, None, :] == token_range[None, :, None], axis=2)
    before = (token_range[:, None] < token_range[None, :]).astype(BF16)
    rank = dot_nn(member.astype(BF16), before).astype(jnp.int32)
    rank = jnp.where(member, rank, -1)
    slot_range = jnp.arange(most, dtype=jnp.int32)
    send_pick = (rank[:, None, :] == slot_range[None, :, None]).astype(BF16)
    send_pick = send_pick.reshape(node_count * most, tok_dev)

    def dispatch(array):
        out = dot_nn(send_pick, array).astype(BF16).reshape(node_count, most, width)
        return lax.all_to_all(out, "expert", 0, 0, tiled=True).reshape(-1, width)

    arrived_rows = dispatch(tokens)
    arrived_grads = dispatch(cotangent)

    own = lax.dynamic_index_in_dim(table, self_index, 0, keepdims=False)
    bounds = jnp.arange(node_count + 1, dtype=jnp.int32) * tok_dev
    starts = jnp.sum((own[:, None] < bounds[None, :]).astype(jnp.int32), axis=0)
    slot_of = starts[:-1, None] + slot_range[None, :]
    slot_of = jnp.where(slot_of < starts[1:, None], slot_of, -1).reshape(-1)
    take_pick = (jnp.arange(slot_count, dtype=jnp.int32)[:, None] == slot_of[None, :]).astype(BF16)

    def halves(array):
        shaped = array.reshape(array.shape[0], chips, 2, block)
        doubled = jnp.concatenate([shaped, shaped], axis=1)

        def part(which):
            start = (jnp.uint32(0), chip, which, jnp.uint32(0))
            taken = lax.dynamic_slice(doubled, start, (array.shape[0], chips, 1, block))
            return taken.reshape(array.shape[0], -1)

        return part(core), part(core ^ 1)

    def both_cores(array):
        keep, give = halves(array)
        return jnp.concatenate([keep, swap_cores(give)], axis=0)

    def all_of_both(array):
        return jnp.concatenate([array, swap_cores(array)], axis=0)

    rows = dot_nn(take_pick, arrived_rows).astype(BF16)
    rows_both = both_cores(rows)
    gate_pre = dot_nn(rows, w_gate[0])
    up_pre = dot_nn(rows, w_up[0])
    sigmoid_gate = jax.nn.sigmoid(gate_pre)
    activated = gate_pre * sigmoid_gate
    hidden = (activated * up_pre).astype(BF16)
    hidden_both = all_of_both(hidden)

    gate_rows = gates[0, 0][:, None]
    grads = dot_nn(take_pick, arrived_grads)
    scaled_grad = (gate_rows * grads).astype(BF16)
    grads = grads.astype(BF16)
    scaled_both = both_cores(scaled_grad)
    down_part = dot_tn(hidden_both, scaled_both).astype(BF16)

    raw_grad = dot_nt(grads, w_down[0])
    slot_grads = jnp.sum(raw_grad * hidden.astype(F32), axis=1)
    hidden_grad = gate_rows * raw_grad
    gate_pre_grad = (
        hidden_grad * up_pre * sigmoid_gate * (1.0 + gate_pre * (1.0 - sigmoid_gate))
    ).astype(BF16)
    up_pre_grad = (hidden_grad * activated).astype(BF16)
    gate_both = all_of_both(gate_pre_grad)
    up_both = all_of_both(up_pre_grad)
    gate_part = dot_tn(rows_both, gate_both).astype(BF16)
    up_part = dot_tn(rows_both, up_both).astype(BF16)

    def row_chunk(part):
        return lambda away: part[away % chips * block : (away % chips + 1) * block]

    def column_chunk(part):
        return lambda away: part[:, away % chips * block : (away % chips + 1) * block]

    half = hidden_width // 2
    grad_down = jnp.concatenate(
        [
            reduce_chunks(column_chunk(down_part[:half]), 1, chips),
            reduce_chunks(column_chunk(down_part[half:]), -1, chips),
        ],
        axis=0,
    )
    grad_gate = reduce_chunks(row_chunk(gate_part), 1, chips)
    grad_up = reduce_chunks(row_chunk(up_part), -1, chips)

    row_grads = (dot_nt(gate_pre_grad, w_gate[0]) + dot_nt(up_pre_grad, w_up[0])).astype(BF16)
    returning = dot_tn(take_pick, row_grads).astype(BF16).reshape(node_count, most, width)
    came_back = lax.all_to_all(returning, "expert", 0, 0, tiled=True).reshape(-1, width)
    token_grads = dot_tn(send_pick, came_back).astype(BF16)
    return (
        token_grads,
        slot_grads[None, None],
        grad_gate[None],
        grad_up[None],
        grad_down[None],
    )


def solution(mesh):
    return jax.shard_map(
        body,
        mesh=mesh,
        in_specs=(
            P(("dp", "expert"), None),
            P(("dp", "expert"), None),
            P("dp", None, None),
            P("dp", "expert", None),
            P("expert", None, None),
            P("expert", None, None),
            P("expert", None, None),
        ),
        out_specs=(
            P(("dp", "expert"), None),
            P("dp", "expert", None),
            P("expert", "dp", None),
            P("expert", "dp", None),
            P("expert", None, "dp"),
        ),
        check_vma=False,
    )
```

```python
import jax
import jax.numpy as jnp
from jax import lax
from jax.experimental import pallas as pl
from jax.experimental.pallas import tpu as pltpu
from jax.sharding import PartitionSpec as P

BF16 = jnp.bfloat16
F32 = jnp.float32
I32 = jnp.int32
VMEM = pl.BlockSpec(memory_space=pltpu.VMEM)
SMEM = pl.BlockSpec(memory_space=pltpu.SMEM)


def dot_nn(left, right):
    return jnp.dot(left, right, preferred_element_type=F32)


def dot_nt(left, right):
    return lax.dot_general(left, right, (((1,), (1,)), ((), ())), preferred_element_type=F32)


def dot_tn(left, right):
    return lax.dot_general(left, right, (((0,), (0,)), ((), ())), preferred_element_type=F32)


def swap_cores(array):
    size = lax.axis_size("dp")
    return lax.ppermute(array, "dp", [(i, i ^ 1) for i in range(size)])


def next_chip(array, sign):
    size = lax.axis_size("dp")
    return lax.ppermute(array, "dp", [(i, (i + 2 * sign) % size) for i in range(size)])


def add(left, right):
    return (left.astype(F32) + right.astype(F32)).astype(BF16)


def two_way_sums(chunk_of, chips, axis):
    far = chips // 2

    def split(chunk):
        return jnp.split(chunk, 2, axis=axis)

    forward = next_chip(split(chunk_of(far))[0], 1)
    backward = next_chip(split(chunk_of(-far))[1], -1)
    for distance in range(far - 1, 0, -1):
        front, back = chunk_of(distance), chunk_of(-distance)
        if distance == far - 1:
            first, second = split(front)
            front = jnp.concatenate([add(forward, first), second], axis=axis)
            first, second = split(back)
            back = jnp.concatenate([first, add(backward, second)], axis=axis)
        else:
            front, back = add(forward, front), add(backward, back)
        forward, backward = next_chip(front, 1), next_chip(back, -1)
    return forward, backward


def finish_sums(own, forward, backward, axis):
    total = own.astype(F32)
    if forward.shape == own.shape:
        return (total + forward.astype(F32) + backward.astype(F32)).astype(BF16)
    arrived = jnp.concatenate([forward, backward], axis=axis)
    return (total + arrived.astype(F32)).astype(BF16)


def select_kernel(most, base_ref, picks_ref, tokens_ref, select_ref, out_ref):
    local = picks_ref[...] - base_ref[0]
    experts, slots = local.shape
    tok_dev = tokens_ref.shape[0]
    below = jnp.sum((local < 0).astype(F32), axis=1, keepdims=True).astype(I32)
    counter = lax.broadcasted_iota(I32, (most, 1), 0)
    spread = jnp.concatenate(
        [jnp.broadcast_to(local[e : e + 1], (most, slots)) for e in range(experts)], axis=0
    )
    wanted = jnp.concatenate([below[e : e + 1] + counter for e in range(experts)], axis=0)
    position = lax.broadcasted_iota(I32, spread.shape, 1)
    hit = (position == wanted) & (spread >= 0) & (spread < tok_dev)
    token = jnp.sum(jnp.where(hit, spread + 1, 0).astype(F32), axis=1, keepdims=True) - 1.0
    token_range = lax.broadcasted_iota(I32, (spread.shape[0], tok_dev), 1).astype(F32)
    select = (token_range == token).astype(F32).astype(BF16)
    select_ref[...] = select
    out_ref[...] = dot_nn(select, tokens_ref[...]).astype(BF16)


def gather_kernel(select_ref, tokens_ref, out_ref):
    out_ref[...] = dot_nn(select_ref[...], tokens_ref[...]).astype(BF16)


def take_kernel(most, tok_dev, own_ref, take_ref):
    slots, columns = take_ref.shape
    lane = lax.broadcasted_iota(I32, (1, columns), 1)
    source = jnp.zeros((1, columns), I32)
    for edge in range(most, columns, most):
        source = source + (lane >= edge).astype(I32)
    within = lane - source * most
    own = own_ref[...]
    start = jnp.sum((own < source * tok_dev).astype(F32), axis=0, keepdims=True)
    stop = jnp.sum((own < (source + 1) * tok_dev).astype(F32), axis=0, keepdims=True)
    slot = start + within.astype(F32)
    slot = jnp.where(slot < stop, slot, -1.0)
    slot_range = lax.broadcasted_iota(I32, (slots, columns), 0).astype(F32)
    take_ref[...] = (slot_range == slot).astype(F32).astype(BF16)


def compact_kernel(chips, place_ref, take_ref, arrived_ref, scale_ref, full_ref, keep_ref, give_ref):
    chip, core = place_ref[0], place_ref[1]
    block = arrived_ref.shape[1] // (2 * chips)
    for k in range(chips):
        columns = slice(2 * k * block, 2 * (k + 1) * block)
        value = dot_nn(take_ref[...], arrived_ref[:, columns])
        full_ref[:, columns] = value.astype(BF16)
        if scale_ref is not None:
            value = value * scale_ref[...]
        value = value.astype(BF16)
        even, odd = value[:, :block], value[:, block:]
        where = pl.ds(pl.multiple_of(lax.rem(k - chip + chips, chips) * block, block), block)

        @pl.when(core == 0)
        def _():
            keep_ref[:, where] = even
            give_ref[:, where] = odd

        @pl.when(core != 0)
        def _():
            keep_ref[:, where] = odd
            give_ref[:, where] = even


def plain_compact_kernel(chips, place_ref, take_ref, arrived_ref, full_ref, keep_ref, give_ref):
    compact_kernel(chips, place_ref, take_ref, arrived_ref, None, full_ref, keep_ref, give_ref)


def call(kernel, out_shapes, in_specs, operands, limit_mib, flops, bytes_accessed):
    return pl.pallas_call(
        kernel,
        out_shape=out_shapes,
        in_specs=in_specs,
        out_specs=jax.tree.map(lambda _: VMEM, out_shapes),
        compiler_params=pltpu.CompilerParams(vmem_limit_bytes=limit_mib * 2**20),
        cost_estimate=pl.CostEstimate(
            flops=flops, bytes_accessed=bytes_accessed, transcendentals=0
        ),
    )(*operands)


def body(tokens, cotangent, picks, gates, w_gate, w_up, w_down):
    node_count = lax.axis_size("expert")
    self_index = lax.axis_index("expert")
    dp_size = lax.axis_size("dp")
    dp_index = lax.axis_index("dp")
    chips = dp_size // 2
    place = jnp.stack([lax.shift_right_logical(dp_index, 1), dp_index & 1]).astype(I32)
    tok_dev, width = tokens.shape
    slot_count = gates.shape[2]
    most = max(2, 3 * slot_count // (2 * node_count))
    padded = node_count * most
    hidden_width = w_gate.shape[2]
    block = width // dp_size

    def shape(*dims, dtype=BF16):
        return jax.ShapeDtypeStruct(dims, dtype)

    table = picks[0]
    base = (self_index * tok_dev).astype(I32).reshape(1)
    select, out_rows = call(
        lambda *refs: select_kernel(most, *refs),
        (shape(padded, tok_dev), shape(padded, width)),
        [SMEM, VMEM, VMEM],
        (base, table, tokens),
        16, 2 * padded * tok_dev * width, 4 * padded * width,
    )
    out_grads = call(
        gather_kernel,
        shape(padded, width),
        [VMEM, VMEM],
        (select, cotangent),
        16, 2 * padded * tok_dev * width, 4 * padded * width,
    )

    def exchange(array):
        shaped = array.reshape(node_count, most, width)
        return lax.all_to_all(shaped, "expert", 0, 0, tiled=True).reshape(padded, width)

    arrived_rows = exchange(out_rows)
    arrived_grads = exchange(out_grads)

    own = lax.dynamic_index_in_dim(table, self_index, 0, keepdims=False)
    take = call(
        lambda *refs: take_kernel(most, tok_dev, *refs),
        shape(slot_count, padded),
        [VMEM],
        (own.reshape(slot_count, 1),),
        8, 8 * slot_count * padded, 2 * slot_count * padded,
    )
    compact_shapes = (
        shape(slot_count, width), shape(slot_count, width // 2), shape(slot_count, width // 2)
    )
    compact_cost = (24, 2 * slot_count * padded * width, 8 * slot_count * width)
    rows, rows_keep, rows_give = call(
        lambda *refs: plain_compact_kernel(chips, *refs),
        compact_shapes,
        [SMEM, VMEM, VMEM],
        (place, take, arrived_rows),
        *compact_cost,
    )
    rows_both = jnp.concatenate([rows_keep, swap_cores(rows_give)], axis=0)
    gate_pre = dot_nn(rows, w_gate[0])
    up_pre = dot_nn(rows, w_up[0])
    sigmoid_gate = jax.nn.sigmoid(gate_pre)
    activated = gate_pre * sigmoid_gate
    slope = up_pre * sigmoid_gate * (1.0 + gate_pre * (1.0 - sigmoid_gate))
    hidden = (activated * up_pre).astype(BF16)
    hidden_both = jnp.concatenate([hidden, swap_cores(hidden)], axis=0)

    gate_rows = gates.reshape(slot_count, 1)
    grads, scaled_keep, scaled_give = call(
        lambda *refs: compact_kernel(chips, *refs),
        compact_shapes,
        [SMEM, VMEM, VMEM, VMEM],
        (place, take, arrived_grads, gate_rows),
        *compact_cost,
    )
    scaled_both = jnp.concatenate([scaled_keep, swap_cores(scaled_give)], axis=0)
    raw_grad = dot_nt(grads, w_down[0])
    slot_grads = jnp.sum(raw_grad * hidden.astype(F32), axis=1)
    hidden_grad = gate_rows * raw_grad
    gate_pre_grad = (hidden_grad * slope).astype(BF16)
    up_pre_grad = (hidden_grad * activated).astype(BF16)
    pre_grads = jnp.concatenate([gate_pre_grad, up_pre_grad], axis=1)
    pre_both = jnp.concatenate([pre_grads, swap_cores(pre_grads)], axis=0)
    down_part = dot_tn(hidden_both, scaled_both).astype(BF16)
    pre_part = dot_tn(rows_both, pre_both).astype(BF16)

    def down_chunk(away):
        return down_part[:, away % chips * block : (away % chips + 1) * block]

    def pre_chunk(away):
        return pre_part[away % chips * block : (away % chips + 1) * block]

    if chips > 1:
        down_sums = two_way_sums(down_chunk, chips, 0)
        pre_sums = two_way_sums(pre_chunk, chips, 1)
        pre_grads, _ = lax.optimization_barrier((pre_grads, pre_part))

    gate_pre_grad, up_pre_grad = jnp.split(pre_grads, 2, axis=1)
    row_grads = (dot_nt(gate_pre_grad, w_gate[0]) + dot_nt(up_pre_grad, w_up[0])).astype(BF16)
    token_grads = dot_tn(select, exchange(dot_tn(take, row_grads).astype(BF16))).astype(BF16)

    if chips > 1:
        token_grads, down_sums, pre_sums = lax.optimization_barrier(
            (token_grads, down_sums, pre_sums)
        )
        grad_down = finish_sums(down_chunk(0), *down_sums, 0)
        grad_pre = finish_sums(pre_chunk(0), *pre_sums, 1)
    else:
        grad_down, grad_pre = down_part, pre_part
    return (
        token_grads,
        slot_grads[None, None],
        grad_pre[None, :, :hidden_width],
        grad_pre[None, :, hidden_width:],
        grad_down[None],
    )


def solution(mesh):
    return jax.shard_map(
        body,
        mesh=mesh,
        in_specs=(
            P(("dp", "expert"), None),
            P(("dp", "expert"), None),
            P("dp", None, None),
            P("dp", "expert", None),
            P("expert", None, None),
            P("expert", None, None),
            P("expert", None, None),
        ),
        out_specs=(
            P(("dp", "expert"), None),
            P("dp", "expert", None),
            P("expert", "dp", None),
            P("expert", "dp", None),
            P("expert", None, "dp"),
        ),
        check_vma=False,
    )
```

```python
import jax
import jax.numpy as jnp
from jax import lax
from jax.experimental import pallas as pl
from jax.experimental.pallas import tpu as pltpu
from jax.sharding import PartitionSpec as P

BF16 = jnp.bfloat16
F32 = jnp.float32
I32 = jnp.int32
VMEM = pl.BlockSpec(memory_space=pltpu.VMEM)
SMEM = pl.BlockSpec(memory_space=pltpu.SMEM)


def dot_nn(left, right):
    return jnp.dot(left, right, preferred_element_type=F32)


def dot_nt(left, right):
    return lax.dot_general(left, right, (((1,), (1,)), ((), ())), preferred_element_type=F32)


def dot_tn(left, right):
    return lax.dot_general(left, right, (((0,), (0,)), ((), ())), preferred_element_type=F32)


def swap_cores(array):
    size = lax.axis_size("dp")
    return lax.ppermute(array, "dp", [(i, i ^ 1) for i in range(size)])


def next_chip(array, sign):
    size = lax.axis_size("dp")
    return lax.ppermute(array, "dp", [(i, (i + 2 * sign) % size) for i in range(size)])


def f32_sum(*terms):
    total = terms[0].astype(F32)
    for term in terms[1:]:
        total = total + term.astype(F32)
    return total.astype(BF16)


def halves_of(shape, axis):
    half = shape[axis] // 2
    full = [slice(None)] * len(shape)
    first, second = list(full), list(full)
    first[axis], second[axis] = slice(0, half), slice(half, 2 * half)
    return tuple(first), tuple(second)


def join_kernel(axis, forward_ref, backward_ref, front_ref, back_ref, front_out, back_out):
    first, second = halves_of(front_ref.shape, axis)
    front_out[first] = f32_sum(forward_ref[...], front_ref[first])
    front_out[second] = front_ref[second]
    back_out[first] = back_ref[first]
    back_out[second] = f32_sum(backward_ref[...], back_ref[second])


def add_kernel(forward_ref, backward_ref, front_ref, back_ref, front_out, back_out):
    front_out[...] = f32_sum(forward_ref[...], front_ref[...])
    back_out[...] = f32_sum(backward_ref[...], back_ref[...])


def finish_kernel(axis, forward_ref, backward_ref, own_ref, *out_refs):
    forward, backward = forward_ref[...], backward_ref[...]
    if forward.shape != own_ref.shape:
        both = jnp.concatenate([forward, backward], axis=axis)
        total = f32_sum(own_ref[...], both)
    else:
        total = f32_sum(own_ref[...], forward, backward)
    for index, out_ref in enumerate(out_refs):
        extent = out_ref.shape[2]
        out_ref[0] = total[:, index * extent : (index + 1) * extent]


class Sums:
    def __init__(self, part, chunk_shape, axis, chips):
        self.part, self.chunk, self.axis, self.chips = part, chunk_shape, axis, chips
        self.across = chunk_shape[0] == part.shape[0]
        self.distance = chips // 2

    def slice(self, away):
        place = away % self.chips
        if self.across:
            return self.part[:, place * self.chunk[1] : (place + 1) * self.chunk[1]]
        return self.part[place * self.chunk[0] : (place + 1) * self.chunk[0]]

    def spec(self, away):
        place = away % self.chips
        return pl.BlockSpec(self.chunk, lambda step: (0, place) if self.across else (place, 0))

    def send(self, front, back):
        self.moving = (next_chip(front, 1), next_chip(back, -1))

    def first(self):
        first, second = halves_of(self.chunk, self.axis)
        chunk = self.slice(self.distance)
        self.send(chunk[first], chunk[second])

    def combine(self, after=None):
        arrived = self.moving
        if after is not None:
            arrived, _ = lax.optimization_barrier((arrived, after))
        kernel = add_kernel
        if self.distance == self.chips // 2:
            kernel = lambda *refs: join_kernel(self.axis, *refs)
        self.distance -= 1
        out = jax.ShapeDtypeStruct(self.chunk, BF16)
        size = self.chunk[0] * self.chunk[1]
        return call(
            kernel,
            (out, out),
            [VMEM, VMEM, self.spec(self.distance), self.spec(-self.distance)],
            (*arrived, self.part, self.part),
            8, 1, 1, (1,),
        )

    def finish(self, out_shapes, after):
        arrived, _ = lax.optimization_barrier((self.moving, after))
        size = self.chunk[0] * self.chunk[1]
        return call(
            lambda *refs: finish_kernel(self.axis, *refs),
            out_shapes,
            [VMEM, VMEM, self.spec(0)],
            (*arrived, self.part),
            8, 1, 1, (1,),
        )


def select_kernel(most, base_ref, picks_ref, tokens_ref, select_ref, turned_ref, out_ref):
    local = picks_ref[...] - base_ref[0]
    experts, slots = local.shape
    tok_dev = tokens_ref.shape[0]
    below = jnp.sum((local < 0).astype(F32), axis=1, keepdims=True).astype(I32)
    counter = lax.broadcasted_iota(I32, (most, 1), 0)
    spread = jnp.concatenate(
        [jnp.broadcast_to(local[e : e + 1], (most, slots)) for e in range(experts)], axis=0
    )
    wanted = jnp.concatenate([below[e : e + 1] + counter for e in range(experts)], axis=0)
    position = lax.broadcasted_iota(I32, spread.shape, 1)
    hit = (position == wanted) & (spread >= 0) & (spread < tok_dev)
    token = jnp.sum(jnp.where(hit, spread + 1, 0).astype(F32), axis=1, keepdims=True) - 1.0
    token_range = lax.broadcasted_iota(I32, (spread.shape[0], tok_dev), 1).astype(F32)
    hot = (token_range == token).astype(F32)
    select = hot.astype(BF16)
    select_ref[...] = select
    turned_ref[...] = hot.T.astype(BF16)
    out_ref[...] = dot_nn(select, tokens_ref[...]).astype(BF16)


def gather_kernel(select_ref, tokens_ref, out_ref):
    out_ref[...] = dot_nn(select_ref[...], tokens_ref[...]).astype(BF16)


def take_kernel(most, tok_dev, own_ref, take_ref, turned_ref):
    slots, columns = take_ref.shape
    lane = lax.broadcasted_iota(I32, (1, columns), 1)
    source = jnp.zeros((1, columns), I32)
    for edge in range(most, columns, most):
        source = source + (lane >= edge).astype(I32)
    within = lane - source * most
    own = own_ref[...]
    start = jnp.sum((own < source * tok_dev).astype(F32), axis=0, keepdims=True)
    stop = jnp.sum((own < (source + 1) * tok_dev).astype(F32), axis=0, keepdims=True)
    slot = start + within.astype(F32)
    slot = jnp.where(slot < stop, slot, -1.0)
    slot_range = lax.broadcasted_iota(I32, (slots, columns), 0).astype(F32)
    hot = (slot_range == slot).astype(F32)
    take_ref[...] = hot.astype(BF16)
    turned_ref[...] = hot.T.astype(BF16)


def compact_kernel(chips, place_ref, take_ref, arrived_ref, scale_ref, full_ref, keep_ref, give_ref):
    chip, core = place_ref[0], place_ref[1]
    block = arrived_ref.shape[1] // (2 * chips)
    for k in range(chips):
        columns = slice(2 * k * block, 2 * (k + 1) * block)
        value = dot_nn(take_ref[...], arrived_ref[:, columns])
        full_ref[:, columns] = value.astype(BF16)
        if scale_ref is not None:
            value = value * scale_ref[...]
        even, odd = value[:, :block], value[:, block:]
        where = pl.ds(pl.multiple_of(lax.rem(k - chip + chips, chips) * block, block), block)

        keep_ref[:, where] = jnp.where(core == 0, even, odd).astype(BF16)
        give_ref[:, where] = jnp.where(core == 0, odd, even).astype(BF16)


def plain_compact_kernel(chips, place_ref, take_ref, arrived_ref, full_ref, keep_ref, give_ref):
    compact_kernel(chips, place_ref, take_ref, arrived_ref, None, full_ref, keep_ref, give_ref)


def grad_kernel(
    tile, grads_ref, down_ref, gate_ref, hidden_ref, slope_ref, activated_ref, pre_ref, slot_ref
):
    hidden_width = down_ref.shape[0]
    total = jnp.zeros(slot_ref.shape, F32)
    for begin in range(0, hidden_width, tile):
        columns = slice(begin, begin + tile)
        raw = dot_nt(grads_ref[...], down_ref[columns, :])
        total = total + jnp.sum(raw * hidden_ref[:, columns].astype(F32), axis=1, keepdims=True)
        scaled = raw * gate_ref[...]
        pre_ref[:, columns] = (scaled * slope_ref[:, columns]).astype(BF16)
        other = slice(hidden_width + begin, hidden_width + begin + tile)
        pre_ref[:, other] = (scaled * activated_ref[:, columns]).astype(BF16)
    slot_ref[...] = total


def return_kernel(tile, pre_ref, gate_ref, up_ref, turned_ref, out_ref):
    width, hidden_width = gate_ref.shape
    for begin in range(0, width, tile):
        columns = slice(begin, begin + tile)
        row_grads = dot_nt(pre_ref[:, :hidden_width], gate_ref[columns, :]) + dot_nt(
            pre_ref[:, hidden_width:], up_ref[columns, :]
        )
        out_ref[:, columns] = dot_nn(turned_ref[...], row_grads.astype(BF16)).astype(BF16)


def call(kernel, out_shapes, in_specs, operands, limit_mib, flops, bytes_accessed, grid=()):
    return pl.pallas_call(
        kernel,
        grid=grid,
        out_shape=out_shapes,
        in_specs=in_specs,
        out_specs=jax.tree.map(lambda _: VMEM, out_shapes),
        compiler_params=pltpu.CompilerParams(vmem_limit_bytes=limit_mib * 2**20),
        cost_estimate=pl.CostEstimate(
            flops=flops, bytes_accessed=bytes_accessed, transcendentals=0
        ),
    )(*operands)


def body(tokens, cotangent, picks, gates, w_gate, w_up, w_down):
    node_count = lax.axis_size("expert")
    self_index = lax.axis_index("expert")
    dp_size = lax.axis_size("dp")
    dp_index = lax.axis_index("dp")
    chips = dp_size // 2
    place = jnp.stack([lax.shift_right_logical(dp_index, 1), dp_index & 1]).astype(I32)
    tok_dev, width = tokens.shape
    slot_count = gates.shape[2]
    most = max(2, 3 * slot_count // (2 * node_count))
    padded = node_count * most
    hidden_width = w_gate.shape[2]
    block = width // dp_size

    def shape(*dims, dtype=BF16):
        return jax.ShapeDtypeStruct(dims, dtype)

    table = picks[0]
    base = (self_index * tok_dev).astype(I32).reshape(1)
    select, select_turned, out_rows = call(
        lambda *refs: select_kernel(most, *refs),
        (shape(padded, tok_dev), shape(tok_dev, padded), shape(padded, width)),
        [SMEM, VMEM, VMEM],
        (base, table, tokens),
        16, 2 * padded * tok_dev * width, 4 * padded * width,
    )
    out_grads = call(
        gather_kernel,
        shape(padded, width),
        [VMEM, VMEM],
        (select, cotangent),
        16, 2 * padded * tok_dev * width, 4 * padded * width,
    )

    def exchange(array):
        shaped = array.reshape(node_count, most, width)
        return lax.all_to_all(shaped, "expert", 0, 0, tiled=True).reshape(padded, width)

    arrived_rows = exchange(out_rows)
    arrived_grads = exchange(out_grads)

    own = lax.dynamic_index_in_dim(table, self_index, 0, keepdims=False)
    take, take_turned = call(
        lambda *refs: take_kernel(most, tok_dev, *refs),
        (shape(slot_count, padded), shape(padded, slot_count)),
        [VMEM],
        (own.reshape(slot_count, 1),),
        8, 8 * slot_count * padded, 2 * slot_count * padded,
    )
    compact_shapes = (
        shape(slot_count, width), shape(slot_count, width // 2), shape(slot_count, width // 2)
    )
    compact_cost = (12, 2 * slot_count * padded * width, 8 * slot_count * width)
    rows, rows_keep, rows_give = call(
        lambda *refs: plain_compact_kernel(chips, *refs),
        compact_shapes,
        [SMEM, VMEM, VMEM],
        (place, take, arrived_rows),
        *compact_cost,
    )
    rows_both = jnp.concatenate([rows_keep, swap_cores(rows_give)], axis=0)
    gate_pre = dot_nn(rows, w_gate[0])
    up_pre = dot_nn(rows, w_up[0])
    sigmoid_gate = jax.nn.sigmoid(gate_pre)
    activated = gate_pre * sigmoid_gate
    slope = up_pre * sigmoid_gate * (1.0 + gate_pre * (1.0 - sigmoid_gate))
    hidden = (activated * up_pre).astype(BF16)
    hidden_both = jnp.concatenate([hidden, swap_cores(hidden)], axis=0)

    gate_rows = gates.reshape(slot_count, 1)
    grads, scaled_keep, scaled_give = call(
        lambda *refs: compact_kernel(chips, *refs),
        compact_shapes,
        [SMEM, VMEM, VMEM, VMEM],
        (place, take, arrived_grads, gate_rows),
        *compact_cost,
    )
    scaled_both = jnp.concatenate([scaled_keep, swap_cores(scaled_give)], axis=0)
    pre_grads, slot_grads = call(
        lambda *refs: grad_kernel(min(256, hidden_width), *refs),
        (shape(slot_count, 2 * hidden_width), shape(slot_count, 1, dtype=F32)),
        [VMEM] * 6,
        (grads, w_down[0], gate_rows, hidden, slope, activated),
        16, 2 * slot_count * width * hidden_width, 2 * width * hidden_width,
    )
    pre_both = jnp.concatenate([pre_grads, swap_cores(pre_grads)], axis=0)
    down_part = dot_tn(hidden_both, scaled_both).astype(BF16)
    pre_part = dot_tn(rows_both, pre_both).astype(BF16)

    def give_back(pre_grads):
        return call(
            lambda *refs: return_kernel(min(256, width), *refs),
            shape(padded, width),
            [VMEM] * 4,
            (pre_grads, w_gate[0], w_up[0], take_turned),
            16, 4 * slot_count * width * hidden_width, 4 * width * hidden_width,
        )

    def collect(came_back):
        return call(
            gather_kernel,
            shape(tok_dev, width),
            [VMEM, VMEM],
            (select_turned, came_back),
            12, 2 * padded * tok_dev * width, 4 * padded * width,
        )

    down_shape = (shape(1, hidden_width, block),)
    pre_shape = (shape(1, block, hidden_width), shape(1, block, hidden_width))
    if chips > 1:
        down = Sums(down_part, (hidden_width, block), 0, chips)
        pre = Sums(pre_part, (block, 2 * hidden_width), 1, chips)
        down.first()
        pre.first()
        returned = None
        held, _ = lax.optimization_barrier((pre_grads, pre_part))
        returning = give_back(held)
        latest = pre_grads
        while down.distance > 1:
            down_next = down.combine(latest)
            if down.distance == chips // 2 - 2:
                returning, _ = lax.optimization_barrier((returning, down_next))
                returned = exchange(returning)
            down.send(*down_next)
            pre_next = pre.combine(down_next)
            pre.send(*pre_next)
            latest = pre_next
        if returned is None:
            returned = exchange(returning)
        returned, _ = lax.optimization_barrier((returned, latest))
        token_grads = collect(returned)
        grad_down = down.finish(down_shape, token_grads)
        grad_pre = pre.finish(pre_shape, token_grads)
    else:
        token_grads = collect(exchange(give_back(pre_grads)))
        grad_down = (down_part[None],)
        grad_pre = tuple(half[None] for half in jnp.split(pre_part, 2, axis=1))
    return (
        token_grads,
        slot_grads.reshape(1, 1, slot_count),
        *grad_pre,
        *grad_down,
    )


def solution(mesh):
    return jax.shard_map(
        body,
        mesh=mesh,
        in_specs=(
            P(("dp", "expert"), None),
            P(("dp", "expert"), None),
            P("dp", None, None),
            P("dp", "expert", None),
            P("expert", None, None),
            P("expert", None, None),
            P("expert", None, None),
        ),
        out_specs=(
            P(("dp", "expert"), None),
            P("dp", "expert", None),
            P("expert", "dp", None),
            P("expert", "dp", None),
            P("expert", None, "dp"),
        ),
        check_vma=False,
    )
```

```python
import jax
import jax.numpy as jnp
from jax import lax
from jax.experimental import pallas as pl
from jax.experimental.pallas import tpu as pltpu
from jax.sharding import PartitionSpec as P

BF16 = jnp.bfloat16
F32 = jnp.float32
I32 = jnp.int32
VMEM = pl.BlockSpec(memory_space=pltpu.VMEM)
SMEM = pl.BlockSpec(memory_space=pltpu.SMEM)


def dot_nn(left, right):
    return jnp.dot(left, right, preferred_element_type=F32)


def dot_nt(left, right):
    return lax.dot_general(left, right, (((1,), (1,)), ((), ())), preferred_element_type=F32)


def dot_tn(left, right):
    return lax.dot_general(left, right, (((0,), (0,)), ((), ())), preferred_element_type=F32)


def swap_cores(array):
    size = lax.axis_size("dp")
    return lax.ppermute(array, "dp", [(i, i ^ 1) for i in range(size)])


def next_chip(array, sign):
    size = lax.axis_size("dp")
    return lax.ppermute(array, "dp", [(i, (i + 2 * sign) % size) for i in range(size)])


def f32_sum(*terms):
    total = terms[0].astype(F32)
    for term in terms[1:]:
        total = total + term.astype(F32)
    return total.astype(BF16)


def chunk_of(pre_ref, down_ref):
    return jnp.concatenate([pre_ref[...], down_ref[...]], axis=1)


def split_kernel(pre_ref, down_ref, front_out, back_out):
    half = front_out.shape[0]
    edge = pre_ref.shape[1]
    for out, rows in ((front_out, slice(0, half)), (back_out, slice(half, 2 * half))):
        out[:, :edge] = pre_ref[rows, :]
        out[:, edge:] = down_ref[rows, :]


def join_kernel(forward_ref, backward_ref, pre_front, down_front, pre_back, down_back, front_out, back_out):
    half = forward_ref.shape[0]
    front, back = chunk_of(pre_front, down_front), chunk_of(pre_back, down_back)
    front_out[:half] = f32_sum(forward_ref[...], front[:half])
    front_out[half:] = front[half:]
    back_out[:half] = back[:half]
    back_out[half:] = f32_sum(backward_ref[...], back[half:])


def add_kernel(forward_ref, backward_ref, pre_front, down_front, pre_back, down_back, front_out, back_out):
    front_out[...] = f32_sum(forward_ref[...], chunk_of(pre_front, down_front))
    back_out[...] = f32_sum(backward_ref[...], chunk_of(pre_back, down_back))


def finish_kernel(forward_ref, backward_ref, pre_ref, down_ref, gate_out, up_out, down_out):
    forward, backward = forward_ref[...], backward_ref[...]
    if forward.shape != gate_out.shape[1:2] + forward.shape[1:]:
        arrived = jnp.concatenate([forward, backward], axis=0).astype(F32)
    else:
        arrived = forward.astype(F32) + backward.astype(F32)
    total = chunk_of(pre_ref, down_ref).astype(F32) + arrived
    hidden = gate_out.shape[2]
    gate_out[0] = total[:, :hidden].astype(BF16)
    up_out[0] = total[:, hidden : 2 * hidden].astype(BF16)
    down_out[0] = total[:, 2 * hidden :].T.astype(BF16)


class Sums:
    def __init__(self, far, parts, block, chips):
        self.parts, self.block, self.chips = parts, block, chips
        self.widths = [part.shape[1] for part in parts]
        self.distance = chips // 2
        half = jax.ShapeDtypeStruct((block // 2, sum(self.widths)), BF16)
        self.send(call(split_kernel, (half, half), [VMEM, VMEM], far, 8, 1, 1))

    def specs(self, away):
        place = away % self.chips
        return [pl.BlockSpec((self.block, width), lambda step: (place, 0)) for width in self.widths]

    def send(self, operands):
        self.moving = (next_chip(operands[0], 1), next_chip(operands[1], -1))

    def step(self):
        kernel = join_kernel if self.distance == self.chips // 2 else add_kernel
        self.distance -= 1
        out = jax.ShapeDtypeStruct((self.block, sum(self.widths)), BF16)
        return call(
            kernel,
            (out, out),
            [VMEM, VMEM, *self.specs(self.distance), *self.specs(-self.distance)],
            (*self.moving, *self.parts, *self.parts),
            12, 1, 1, (1,),
        )

    def finish(self, out_shapes, after):
        arrived, _ = lax.optimization_barrier((self.moving, after))
        return call(
            finish_kernel,
            out_shapes,
            [VMEM, VMEM, *self.specs(0)],
            (*arrived, *self.parts),
            12, 1, 1, (1,),
        )


def select_kernel(most, base_ref, picks_ref, tokens_ref, select_ref, turned_ref, out_ref):
    local = picks_ref[...] - base_ref[0]
    experts, slots = local.shape
    tok_dev = tokens_ref.shape[0]
    below = jnp.sum((local < 0).astype(F32), axis=1, keepdims=True).astype(I32)
    counter = lax.broadcasted_iota(I32, (most, 1), 0)
    spread = jnp.concatenate(
        [jnp.broadcast_to(local[e : e + 1], (most, slots)) for e in range(experts)], axis=0
    )
    wanted = jnp.concatenate([below[e : e + 1] + counter for e in range(experts)], axis=0)
    position = lax.broadcasted_iota(I32, spread.shape, 1)
    hit = (position == wanted) & (spread >= 0) & (spread < tok_dev)
    token = jnp.sum(jnp.where(hit, spread + 1, 0).astype(F32), axis=1, keepdims=True) - 1.0
    token_range = lax.broadcasted_iota(I32, (spread.shape[0], tok_dev), 1).astype(F32)
    hot = (token_range == token).astype(F32)
    select = hot.astype(BF16)
    select_ref[...] = select
    turned_ref[...] = hot.T.astype(BF16)
    out_ref[...] = dot_nn(select, tokens_ref[...]).astype(BF16)


def gather_kernel(select_ref, tokens_ref, out_ref):
    out_ref[...] = dot_nn(select_ref[...], tokens_ref[...]).astype(BF16)


def take_kernel(most, tok_dev, own_ref, take_ref, turned_ref):
    slots, columns = take_ref.shape
    lane = lax.broadcasted_iota(I32, (1, columns), 1)
    source = jnp.zeros((1, columns), I32)
    for edge in range(most, columns, most):
        source = source + (lane >= edge).astype(I32)
    within = lane - source * most
    own = own_ref[...]
    start = jnp.sum((own < source * tok_dev).astype(F32), axis=0, keepdims=True)
    stop = jnp.sum((own < (source + 1) * tok_dev).astype(F32), axis=0, keepdims=True)
    slot = start + within.astype(F32)
    slot = jnp.where(slot < stop, slot, -1.0)
    slot_range = lax.broadcasted_iota(I32, (slots, columns), 0).astype(F32)
    hot = (slot_range == slot).astype(F32)
    take_ref[...] = hot.astype(BF16)
    turned_ref[...] = hot.T.astype(BF16)


def compact_kernel(chips, place_ref, take_ref, arrived_ref, scale_ref, full_ref, keep_ref, give_ref):
    chip, core = place_ref[0], place_ref[1]
    block = arrived_ref.shape[1] // (2 * chips)
    for k in range(chips):
        columns = slice(2 * k * block, 2 * (k + 1) * block)
        value = dot_nn(take_ref[...], arrived_ref[:, columns])
        full_ref[:, columns] = value.astype(BF16)
        if scale_ref is not None:
            value = value * scale_ref[...]
        even, odd = value[:, :block], value[:, block:]
        where = pl.ds(pl.multiple_of(lax.rem(k - chip + chips, chips) * block, block), block)

        keep_ref[:, where] = jnp.where(core == 0, even, odd).astype(BF16)
        give_ref[:, where] = jnp.where(core == 0, odd, even).astype(BF16)


def plain_compact_kernel(chips, place_ref, take_ref, arrived_ref, full_ref, keep_ref, give_ref):
    compact_kernel(chips, place_ref, take_ref, arrived_ref, None, full_ref, keep_ref, give_ref)


def grad_kernel(
    tile, grads_ref, down_ref, gate_ref, hidden_ref, slope_ref, activated_ref, pre_ref, slot_ref
):
    hidden_width = down_ref.shape[0]
    total = jnp.zeros(slot_ref.shape, F32)
    for begin in range(0, hidden_width, tile):
        columns = slice(begin, begin + tile)
        raw = dot_nt(grads_ref[...], down_ref[columns, :])
        total = total + jnp.sum(raw * hidden_ref[:, columns].astype(F32), axis=1, keepdims=True)
        scaled = raw * gate_ref[...]
        pre_ref[:, columns] = (scaled * slope_ref[:, columns]).astype(BF16)
        other = slice(hidden_width + begin, hidden_width + begin + tile)
        pre_ref[:, other] = (scaled * activated_ref[:, columns]).astype(BF16)
    slot_ref[...] = total


def return_kernel(tile, pre_ref, gate_ref, up_ref, turned_ref, out_ref):
    width, hidden_width = gate_ref.shape
    for begin in range(0, width, tile):
        columns = slice(begin, begin + tile)
        row_grads = dot_nt(pre_ref[:, :hidden_width], gate_ref[columns, :]) + dot_nt(
            pre_ref[:, hidden_width:], up_ref[columns, :]
        )
        out_ref[:, columns] = dot_nn(turned_ref[...], row_grads.astype(BF16)).astype(BF16)


def call(kernel, out_shapes, in_specs, operands, limit_mib, flops, bytes_accessed, grid=()):
    return pl.pallas_call(
        kernel,
        grid=grid,
        out_shape=out_shapes,
        in_specs=in_specs,
        out_specs=jax.tree.map(lambda _: VMEM, out_shapes),
        compiler_params=pltpu.CompilerParams(vmem_limit_bytes=limit_mib * 2**20),
        cost_estimate=pl.CostEstimate(
            flops=flops, bytes_accessed=bytes_accessed, transcendentals=0
        ),
    )(*operands)


def body(tokens, cotangent, picks, gates, w_gate, w_up, w_down):
    node_count = lax.axis_size("expert")
    self_index = lax.axis_index("expert")
    dp_size = lax.axis_size("dp")
    dp_index = lax.axis_index("dp")
    chips = dp_size // 2
    place = jnp.stack([lax.shift_right_logical(dp_index, 1), dp_index & 1]).astype(I32)
    tok_dev, width = tokens.shape
    slot_count = gates.shape[2]
    most = max(2, 3 * slot_count // (2 * node_count))
    padded = node_count * most
    hidden_width = w_gate.shape[2]
    block = width // dp_size

    def shape(*dims, dtype=BF16):
        return jax.ShapeDtypeStruct(dims, dtype)

    table = picks[0]
    base = (self_index * tok_dev).astype(I32).reshape(1)
    select, select_turned, out_rows = call(
        lambda *refs: select_kernel(most, *refs),
        (shape(padded, tok_dev), shape(tok_dev, padded), shape(padded, width)),
        [SMEM, VMEM, VMEM],
        (base, table, tokens),
        16, 2 * padded * tok_dev * width, 4 * padded * width,
    )
    out_grads = call(
        gather_kernel,
        shape(padded, width),
        [VMEM, VMEM],
        (select, cotangent),
        16, 2 * padded * tok_dev * width, 4 * padded * width,
    )

    def exchange(array):
        shaped = array.reshape(node_count, most, width)
        return lax.all_to_all(shaped, "expert", 0, 0, tiled=True).reshape(padded, width)

    arrived_rows = exchange(out_rows)
    arrived_grads = exchange(out_grads)

    own = lax.dynamic_index_in_dim(table, self_index, 0, keepdims=False)
    take, take_turned = call(
        lambda *refs: take_kernel(most, tok_dev, *refs),
        (shape(slot_count, padded), shape(padded, slot_count)),
        [VMEM],
        (own.reshape(slot_count, 1),),
        8, 8 * slot_count * padded, 2 * slot_count * padded,
    )
    compact_shapes = (
        shape(slot_count, width), shape(slot_count, width // 2), shape(slot_count, width // 2)
    )
    compact_cost = (12, 2 * slot_count * padded * width, 8 * slot_count * width)
    rows, rows_keep, rows_give = call(
        lambda *refs: plain_compact_kernel(chips, *refs),
        compact_shapes,
        [SMEM, VMEM, VMEM],
        (place, take, arrived_rows),
        *compact_cost,
    )
    rows_both = jnp.concatenate([rows_keep, swap_cores(rows_give)], axis=0)
    gate_pre = dot_nn(rows, w_gate[0])
    up_pre = dot_nn(rows, w_up[0])
    sigmoid_gate = jax.nn.sigmoid(gate_pre)
    activated = gate_pre * sigmoid_gate
    slope = up_pre * sigmoid_gate * (1.0 + gate_pre * (1.0 - sigmoid_gate))
    hidden = (activated * up_pre).astype(BF16)
    hidden_both = jnp.concatenate([hidden, swap_cores(hidden)], axis=0)

    gate_rows = gates.reshape(slot_count, 1)
    arrived_grads, hidden, slope, activated, rows_both, hidden_both = lax.optimization_barrier(
        (arrived_grads, hidden, slope, activated, rows_both, hidden_both)
    )
    grads, scaled_keep, scaled_give = call(
        lambda *refs: compact_kernel(chips, *refs),
        compact_shapes,
        [SMEM, VMEM, VMEM, VMEM],
        (place, take, arrived_grads, gate_rows),
        *compact_cost,
    )
    scaled_both = jnp.concatenate([scaled_keep, swap_cores(scaled_give)], axis=0)
    pre_grads, slot_grads = call(
        lambda *refs: grad_kernel(min(256, hidden_width), *refs),
        (shape(slot_count, 2 * hidden_width), shape(slot_count, 1, dtype=F32)),
        [VMEM] * 6,
        (grads, w_down[0], gate_rows, hidden, slope, activated),
        16, 2 * slot_count * width * hidden_width, 2 * width * hidden_width,
    )
    pre_both = jnp.concatenate([pre_grads, swap_cores(pre_grads)], axis=0)

    def parts_of(columns):
        return (
            dot_tn(rows_both[:, columns], pre_both).astype(BF16),
            dot_tn(scaled_both[:, columns], hidden_both).astype(BF16),
        )

    def give_back(pre_grads):
        return call(
            lambda *refs: return_kernel(min(256, width), *refs),
            shape(padded, width),
            [VMEM] * 4,
            (pre_grads, w_gate[0], w_up[0], take_turned),
            16, 4 * slot_count * width * hidden_width, 4 * width * hidden_width,
        )

    def collect(came_back):
        return call(
            gather_kernel,
            shape(tok_dev, width),
            [VMEM, VMEM],
            (select_turned, came_back),
            12, 2 * padded * tok_dev * width, 4 * padded * width,
        )

    if chips > 1:
        farthest = chips // 2
        far = parts_of(slice(farthest * block, (farthest + 1) * block))
        parts = parts_of(slice(None))
        sums = Sums(far, parts, block, chips)
        returning = give_back(pre_grads)
        returned = None
        while sums.distance > 1:
            operands = sums.step()
            if returned is None:
                returning, _ = lax.optimization_barrier((returning, operands))
                returned = exchange(returning)
            sums.send(operands)
            latest = operands
        if returned is None:
            returned, latest = exchange(returning), returning
        returned, _ = lax.optimization_barrier((returned, latest))
        token_grads = collect(returned)
        weight_shapes = (
            shape(1, block, hidden_width),
            shape(1, block, hidden_width),
            shape(1, hidden_width, block),
        )
        weight_grads = sums.finish(weight_shapes, token_grads)
    else:
        token_grads = collect(exchange(give_back(pre_grads)))
        pre_part, down_part = parts_of(slice(None))
        weight_grads = (*(half[None] for half in jnp.split(pre_part, 2, axis=1)), down_part.T[None])
    return (token_grads, slot_grads.reshape(1, 1, slot_count), *weight_grads)


def solution(mesh):
    return jax.shard_map(
        body,
        mesh=mesh,
        in_specs=(
            P(("dp", "expert"), None),
            P(("dp", "expert"), None),
            P("dp", None, None),
            P("dp", "expert", None),
            P("expert", None, None),
            P("expert", None, None),
            P("expert", None, None),
        ),
        out_specs=(
            P(("dp", "expert"), None),
            P("dp", "expert", None),
            P("expert", "dp", None),
            P("expert", "dp", None),
            P("expert", None, "dp"),
        ),
        check_vma=False,
    )
```

```python
import functools

import jax
import jax.numpy as jnp
from jax import lax
from jax.experimental import pallas as pl
from jax.experimental.pallas import tpu as pltpu
from jax.sharding import PartitionSpec as P

BF16 = jnp.bfloat16
F32 = jnp.float32
I32 = jnp.int32
VMEM = pl.BlockSpec(memory_space=pltpu.VMEM)
SMEM = pl.BlockSpec(memory_space=pltpu.SMEM)


def dot_nn(left, right):
    return jnp.dot(left, right, preferred_element_type=F32)


def dot_nt(left, right):
    return lax.dot_general(left, right, (((1,), (1,)), ((), ())), preferred_element_type=F32)


def dot_tn(left, right):
    return lax.dot_general(left, right, (((0,), (0,)), ((), ())), preferred_element_type=F32)


def swap_cores(array):
    size = lax.axis_size("dp")
    return lax.ppermute(array, "dp", [(i, i ^ 1) for i in range(size)])


def next_chip(array, sign):
    size = lax.axis_size("dp")
    return lax.ppermute(array, "dp", [(i, (i + 2 * sign) % size) for i in range(size)])


def along(array, axis, shift, side):
    pairs = []
    for source in range(side * side):
        spot = [source // side, source % side]
        spot[axis] = (spot[axis] + shift) % side
        pairs.append((source, spot[0] * side + spot[1]))
    return lax.ppermute(array, "expert", pairs)


def restack_kernel(group, *refs):
    count = len(refs) // 2
    for a in range(count):
        for b in range(count):
            refs[count + b][a * group : (a + 1) * group] = refs[a][b * group : (b + 1) * group]


def first_phase(messages, axis, side):
    return [messages[0]] + [along(messages[p], axis, p, side) for p in range(1, side)]


def second_phase(arrived, axis, side, group):
    same = tuple(jax.ShapeDtypeStruct(item.shape, item.dtype) for item in arrived)
    size = 4 * side * arrived[0].size
    pieces = call(
        lambda *refs: restack_kernel(group, *refs), same, [VMEM] * side, arrived, 8, 1, size
    )
    return [pieces[0]] + [along(pieces[q], 1 - axis, q, side) for q in range(1, side)]


def peer(place_ref, side, axis, sign, p, q):
    dx, dy = (p, q) if axis == 0 else (q, p)
    if sign < 0:
        dx, dy = side - dx, side - dy
    return ((place_ref[0] + dx) & (side - 1)) * side + ((place_ref[1] + dy) & (side - 1))


def f32_sum(*terms):
    total = terms[0].astype(F32)
    for term in terms[1:]:
        total = total + term.astype(F32)
    return total.astype(BF16)


def chunk_of(pre_ref, down_ref):
    return jnp.concatenate([pre_ref[...], down_ref[...]], axis=1)


def split_kernel(pre_ref, down_ref, front_out, back_out):
    half = front_out.shape[0]
    edge = pre_ref.shape[1]
    for out, rows in ((front_out, slice(0, half)), (back_out, slice(half, 2 * half))):
        out[:, :edge] = pre_ref[rows, :]
        out[:, edge:] = down_ref[rows, :]


def join_kernel(forward_ref, backward_ref, pre_front, down_front, pre_back, down_back, front_out, back_out):
    half = forward_ref.shape[0]
    front, back = chunk_of(pre_front, down_front), chunk_of(pre_back, down_back)
    front_out[:half] = f32_sum(forward_ref[...], front[:half])
    front_out[half:] = front[half:]
    back_out[:half] = back[:half]
    back_out[half:] = f32_sum(backward_ref[...], back[half:])


def add_kernel(forward_ref, backward_ref, pre_front, down_front, pre_back, down_back, front_out, back_out):
    front_out[...] = f32_sum(forward_ref[...], chunk_of(pre_front, down_front))
    back_out[...] = f32_sum(backward_ref[...], chunk_of(pre_back, down_back))


def finish_kernel(forward_ref, backward_ref, pre_ref, down_ref, gate_out, up_out, down_out):
    forward, backward = forward_ref[...], backward_ref[...]
    if forward.shape != gate_out.shape[1:2] + forward.shape[1:]:
        arrived = jnp.concatenate([forward, backward], axis=0).astype(F32)
    else:
        arrived = forward.astype(F32) + backward.astype(F32)
    total = chunk_of(pre_ref, down_ref).astype(F32) + arrived
    hidden = gate_out.shape[2]
    gate_out[0] = total[:, :hidden].astype(BF16)
    up_out[0] = total[:, hidden : 2 * hidden].astype(BF16)
    down_out[0] = total[:, 2 * hidden :].T.astype(BF16)


class Sums:
    def __init__(self, far, parts, block, chips):
        self.parts, self.block, self.chips = parts, block, chips
        self.widths = [part.shape[1] for part in parts]
        self.distance = chips // 2
        half = jax.ShapeDtypeStruct((block // 2, sum(self.widths)), BF16)
        self.send(call(split_kernel, (half, half), [VMEM, VMEM], far, 8, 1, 1))

    def specs(self, away):
        place = away % self.chips
        return [pl.BlockSpec((self.block, width), lambda step: (place, 0)) for width in self.widths]

    def send(self, operands):
        self.moving = (next_chip(operands[0], 1), next_chip(operands[1], -1))

    def step(self):
        kernel = join_kernel if self.distance == self.chips // 2 else add_kernel
        self.distance -= 1
        out = jax.ShapeDtypeStruct((self.block, sum(self.widths)), BF16)
        return call(
            kernel,
            (out, out),
            [VMEM, VMEM, *self.specs(self.distance), *self.specs(-self.distance)],
            (*self.moving, *self.parts, *self.parts),
            12, 1, 1, (1,),
        )

    def finish(self, out_shapes, after):
        arrived, _ = lax.optimization_barrier((self.moving, after))
        return call(
            finish_kernel,
            out_shapes,
            [VMEM, VMEM, *self.specs(0)],
            (*arrived, *self.parts),
            12, 1, 1, (1,),
        )


def select_matrix(side, most, axis, sign, place_ref, picks_ref, tok_dev):
    base = place_ref[4]
    slots = picks_ref.shape[1]
    order = [(p, q) for p in range(side) for q in range(side)]
    if sign < 0:
        order = [(p, q) for q in range(side) for p in range(side)]
    spread = jnp.concatenate(
        [
            jnp.broadcast_to(
                picks_ref[pl.ds(peer(place_ref, side, axis, sign, p, q), 1), :], (2 * most, slots)
            )
            for p, q in order
        ],
        axis=0,
    )
    local = spread - base
    within = lax.broadcasted_iota(I32, (2 * most, 1), 0)
    second = (within >= most).astype(I32)
    counter = jnp.concatenate([within - most * second] * len(order), axis=0)
    second = jnp.concatenate([second] * len(order), axis=0).astype(F32)
    below = jnp.sum((local < 0).astype(F32), axis=1, keepdims=True).astype(I32)
    position = lax.broadcasted_iota(I32, local.shape, 1)
    hit = (position == below + counter) & (local >= 0) & (local < tok_dev)
    token = jnp.sum(jnp.where(hit, local + 1, 0).astype(F32), axis=1, keepdims=True) - 1.0
    token_range = lax.broadcasted_iota(I32, (local.shape[0], tok_dev), 1).astype(F32)
    hot = (token_range == token).astype(F32)
    return jnp.concatenate([hot * (1.0 - second), hot * second], axis=1)


def send_kernel(side, most, axis, columns, place_ref, picks_ref, tokens_ref, cotangent_ref, *out_refs):
    select = select_matrix(side, most, axis, 1, place_ref, picks_ref, tokens_ref.shape[0])
    both = jnp.concatenate([tokens_ref[:, columns], cotangent_ref[:, columns]], axis=0)
    value = dot_nn(select.astype(BF16), both).astype(BF16)
    rows = value.shape[0] // side
    for index, out_ref in enumerate(out_refs):
        out_ref[...] = value[index * rows : (index + 1) * rows]


def collect_matrix_kernel(side, most, place_ref, picks_ref, *out_refs):
    for axis, out_ref in enumerate(out_refs):
        tok_dev = out_ref.shape[0] // 2
        select = select_matrix(side, most, axis, -1, place_ref, picks_ref, tok_dev)
        out_ref[...] = select.T.astype(BF16)


def take_matrix(side, most, tok_dev, axis, sign, place_ref, own_ref):
    slots = own_ref.shape[0]
    columns = 2 * most * side * side
    lane = lax.broadcasted_iota(I32, (1, columns), 1)
    half = jnp.zeros((1, columns), I32)
    for edge in range(most, columns, most):
        half = half + (lane >= edge).astype(I32)
    within = lane - half * most
    group = half >> 1
    low = group & (side - 1)
    high = group >> (side.bit_length() - 1)
    p, q = (high, low) if sign > 0 else (low, high)
    source = peer(place_ref, side, axis, sign, p, q)
    own = own_ref[...]
    start = jnp.sum((own < source * tok_dev).astype(F32), axis=0, keepdims=True)
    stop = jnp.sum((own < (source + 1) * tok_dev).astype(F32), axis=0, keepdims=True)
    slot = start + within.astype(F32)
    slot = jnp.where(slot < stop, slot, -1.0)
    slot_range = lax.broadcasted_iota(I32, (slots, columns), 0).astype(F32)
    hot = (slot_range == slot).astype(F32)
    second = (half & 1).astype(F32)
    return jnp.concatenate([hot * (1.0 - second), hot * second], axis=0)


def take_kernel(side, most, tok_dev, place_ref, own_ref, *out_refs):
    for axis in range(2):
        take = take_matrix(side, most, tok_dev, axis, -1, place_ref, own_ref)
        out_refs[axis][...] = take.astype(BF16)
        give = take_matrix(side, most, tok_dev, axis, 1, place_ref, own_ref)
        out_refs[2 + axis][...] = give.T.astype(BF16)


def compact_kernel(side, chips, place_ref, gate_ref, *refs):
    takes, pieces = refs[:2], refs[2 : 2 + 2 * side]
    rows_ref, rows_keep, rows_give, grads_ref, scaled_keep, scaled_give = refs[2 + 2 * side :]
    chip, core = place_ref[2], place_ref[3]
    slots, width = rows_ref.shape
    block = width // (2 * chips)
    per_route = max(1, chips // 2)
    for k in range(chips):
        route = k // per_route if chips > 1 else 0
        begin = 2 * (k - route * per_route) * block
        local = slice(begin, begin + 2 * block)
        columns = slice(2 * k * block, 2 * (k + 1) * block)
        arrived = jnp.concatenate(
            [piece[:, local] for piece in pieces[route * side : (route + 1) * side]], axis=0
        )
        both = dot_nn(takes[route][...], arrived)
        where = pl.ds(pl.multiple_of(lax.rem(k - chip + chips, chips) * block, block), block)
        rows, grads = both[:slots], both[slots:]
        rows_ref[:, columns] = rows.astype(BF16)
        grads_ref[:, columns] = grads.astype(BF16)
        for value, keep_ref, give_ref in (
            (rows, rows_keep, rows_give), (grads * gate_ref[...], scaled_keep, scaled_give)
        ):
            even, odd = value[:, :block], value[:, block:]
            keep_ref[:, where] = jnp.where(core == 0, even, odd).astype(BF16)
            give_ref[:, where] = jnp.where(core == 0, odd, even).astype(BF16)


def expert_kernel(
    tile, rows_ref, grads_ref, gate_ref, up_ref, down_ref, scale_ref, pre_ref, hidden_ref, slot_ref
):
    hidden_width = down_ref.shape[0]
    total = jnp.zeros(slot_ref.shape, F32)
    for begin in range(0, hidden_width, tile):
        columns = slice(begin, begin + tile)
        gate_pre = dot_nn(rows_ref[...], gate_ref[:, columns])
        up_pre = dot_nn(rows_ref[...], up_ref[:, columns])
        raw = dot_nt(grads_ref[...], down_ref[columns, :])
        sigmoid_gate = jax.nn.sigmoid(gate_pre)
        activated = gate_pre * sigmoid_gate
        hidden = (activated * up_pre).astype(BF16)
        hidden_ref[:, columns] = hidden
        total = total + jnp.sum(raw * hidden.astype(F32), axis=1, keepdims=True)
        scaled = raw * scale_ref[...]
        slope = up_pre * sigmoid_gate * (1.0 + gate_pre * (1.0 - sigmoid_gate))
        pre_ref[:, columns] = (scaled * slope).astype(BF16)
        other = slice(hidden_width + begin, hidden_width + begin + tile)
        pre_ref[:, other] = (scaled * activated).astype(BF16)
    slot_ref[...] = total


def return_kernel(tile, pre_ref, gate_ref, up_ref, *refs):
    gives, outs, held = refs[:2], refs[2:-1], refs[-1]
    width, hidden_width = gate_ref.shape
    for begin in range(0, width, tile):
        columns = slice(begin, begin + tile)
        row_grads = dot_nt(pre_ref[:, :hidden_width], gate_ref[columns, :]) + dot_nt(
            pre_ref[:, hidden_width:], up_ref[columns, :]
        )
        held[:, columns] = row_grads.astype(BF16)
    quarter = width // 4
    side = len(outs) // 2
    for route in range(2):
        begin = 2 * route * quarter
        both = jnp.concatenate(
            [held[:, begin : begin + quarter], held[:, begin + quarter : begin + 2 * quarter]], axis=0
        )
        value = dot_nn(gives[route][...], both).astype(BF16)
        rows = value.shape[0] // side
        for index in range(side):
            outs[route * side + index][...] = value[index * rows : (index + 1) * rows]


def collect_kernel(side, *refs):
    matrices, pieces, out_ref = refs[:2], refs[2:-1], refs[-1]
    tok_dev, width = out_ref.shape
    quarter = width // 4
    for route in range(2):
        arrived = jnp.concatenate(
            [piece[...] for piece in pieces[route * side : (route + 1) * side]], axis=0
        )
        value = dot_nn(matrices[route][...], arrived).astype(BF16)
        begin = 2 * route * quarter
        out_ref[:, begin : begin + quarter] = value[:tok_dev]
        out_ref[:, begin + quarter : begin + 2 * quarter] = value[tok_dev:]


def call(kernel, out_shapes, in_specs, operands, limit_mib, flops, bytes_accessed, grid=(), scratch=()):
    return pl.pallas_call(
        kernel,
        grid=grid,
        out_shape=out_shapes,
        in_specs=in_specs,
        out_specs=jax.tree.map(lambda _: VMEM, out_shapes),
        scratch_shapes=scratch,
        compiler_params=pltpu.CompilerParams(vmem_limit_bytes=limit_mib * 2**20),
        cost_estimate=pl.CostEstimate(
            flops=flops, bytes_accessed=bytes_accessed, transcendentals=0
        ),
    )(*operands)


def body(tokens, cotangent, picks, gates, w_gate, w_up, w_down):
    node_count = lax.axis_size("expert")
    self_index = lax.axis_index("expert")
    dp_size = lax.axis_size("dp")
    dp_index = lax.axis_index("dp")
    chips = dp_size // 2
    tok_dev, width = tokens.shape
    slot_count = gates.shape[2]
    most = max(2, 3 * slot_count // (2 * node_count))
    hidden_width = w_gate.shape[2]
    block = width // dp_size
    side = 1 << (node_count.bit_length() // 2)
    group = 2 * most
    message = side * group
    place = jnp.stack(
        [
            lax.shift_right_logical(self_index, side.bit_length() - 1),
            self_index & (side - 1),
            lax.shift_right_logical(dp_index, 1),
            dp_index & 1,
            self_index * tok_dev,
        ]
    ).astype(I32)

    def shape(*dims, dtype=BF16):
        return jax.ShapeDtypeStruct(dims, dtype)

    table = picks[0]
    own = lax.dynamic_index_in_dim(table, self_index, 0, keepdims=False).reshape(slot_count, 1)
    gate_rows = gates.reshape(slot_count, 1)

    arrived = []
    for axis in range(2):
        columns = slice(axis * width // 2, (axis + 1) * width // 2)
        messages = call(
            functools.partial(send_kernel, side, most, axis, columns),
            (shape(message, width // 2),) * side,
            [SMEM, VMEM, VMEM, VMEM],
            (place, table, tokens, cotangent),
            12, 2 * message * side * tok_dev * width, 4 * message * side * width,
        )
        arrived += second_phase(first_phase(messages, axis, side), axis, side, group)

    takes = call(
        functools.partial(take_kernel, side, most, tok_dev),
        (shape(2 * slot_count, message * side),) * 2 + (shape(message * side, 2 * slot_count),) * 2,
        [SMEM, VMEM],
        (place, own),
        12, 32 * slot_count * message * side, 16 * slot_count * message * side,
    )
    collects = call(
        functools.partial(collect_matrix_kernel, side, most),
        (shape(2 * tok_dev, message * side),) * 2,
        [SMEM, VMEM],
        (place, table),
        12, 32 * slot_count * message * side, 8 * slot_count * message * side,
    )

    whole, part = shape(slot_count, width), shape(slot_count, width // 2)
    rows, rows_keep, rows_give, grads, scaled_keep, scaled_give = call(
        functools.partial(compact_kernel, side, chips),
        (whole, part, part, whole, part, part),
        [SMEM] + [VMEM] * (3 + 2 * side),
        (place, gate_rows, *takes[:2], *arrived),
        12, 4 * slot_count * message * side * width, 16 * slot_count * width,
    )
    pre_grads, hidden, slot_grads = call(
        functools.partial(expert_kernel, min(256, hidden_width)),
        (
            shape(slot_count, 2 * hidden_width),
            shape(slot_count, hidden_width),
            shape(slot_count, 1, dtype=F32),
        ),
        [VMEM] * 6,
        (rows, grads, w_gate[0], w_up[0], w_down[0], gate_rows),
        12, 6 * slot_count * width * hidden_width, 6 * width * hidden_width,
    )
    rows_both = jnp.concatenate([rows_keep, swap_cores(rows_give)], axis=0)
    scaled_both = jnp.concatenate([scaled_keep, swap_cores(scaled_give)], axis=0)
    hidden_both = jnp.concatenate([hidden, swap_cores(hidden)], axis=0)
    pre_both = jnp.concatenate([pre_grads, swap_cores(pre_grads)], axis=0)

    def parts_of(columns):
        return (
            dot_tn(rows_both[:, columns], pre_both).astype(BF16),
            dot_tn(scaled_both[:, columns], hidden_both).astype(BF16),
        )

    def give_back(pre_grads):
        return call(
            functools.partial(return_kernel, min(256, width)),
            (shape(message, width // 4),) * (2 * side),
            [VMEM] * 5,
            (pre_grads, w_gate[0], w_up[0], *takes[2:]),
            12, 4 * slot_count * width * hidden_width, 4 * width * hidden_width,
            scratch=(pltpu.VMEM((slot_count, width), BF16),),
        )

    def go_back(returning):
        return [
            first_phase(returning[axis * side : (axis + 1) * side], axis, side) for axis in range(2)
        ]

    def turn(arrived):
        return second_phase(arrived[0], 0, side, group) + second_phase(arrived[1], 1, side, group)

    def collect(came_back):
        return call(
            functools.partial(collect_kernel, side),
            shape(tok_dev, width),
            [VMEM] * (2 + 2 * side),
            (*collects, *came_back),
            8, 2 * message * side * tok_dev * width, 4 * message * side * width,
        )

    if chips > 1:
        farthest = chips // 2
        far = parts_of(slice(farthest * block, (farthest + 1) * block))
        parts = parts_of(slice(None))
        sums = Sums(far, parts, block, chips)
        back = give_back(pre_grads)
        stages = [go_back, turn, collect]
        while sums.distance > 1:
            sums.moving, back = lax.optimization_barrier((sums.moving, back))
            operands = sums.step()
            sums.send(operands)
            if len(stages) > 1:
                back = stages.pop(0)(back)
        for stage in stages:
            back, _ = lax.optimization_barrier((back, operands))
            back = stage(back)
        token_grads = back
        weight_shapes = (
            shape(1, block, hidden_width),
            shape(1, block, hidden_width),
            shape(1, hidden_width, block),
        )
        weight_grads = sums.finish(weight_shapes, token_grads)
    else:
        token_grads = collect(turn(go_back(give_back(pre_grads))))
        pre_part, down_part = parts_of(slice(None))
        weight_grads = (*(half[None] for half in jnp.split(pre_part, 2, axis=1)), down_part.T[None])
    return (token_grads, slot_grads.reshape(1, 1, slot_count), *weight_grads)


def solution(mesh):
    return jax.shard_map(
        body,
        mesh=mesh,
        in_specs=(
            P(("dp", "expert"), None),
            P(("dp", "expert"), None),
            P("dp", None, None),
            P("dp", "expert", None),
            P("expert", None, None),
            P("expert", None, None),
            P("expert", None, None),
        ),
        out_specs=(
            P(("dp", "expert"), None),
            P("dp", "expert", None),
            P("expert", "dp", None),
            P("expert", "dp", None),
            P("expert", None, "dp"),
        ),
        check_vma=False,
    )
```

```python
import functools

import jax
import jax.numpy as jnp
from jax import lax
from jax.experimental import pallas as pl
from jax.experimental.pallas import tpu as pltpu
from jax.sharding import PartitionSpec as P

BF16 = jnp.bfloat16
F32 = jnp.float32
I32 = jnp.int32
VMEM = pl.BlockSpec(memory_space=pltpu.VMEM)
SMEM = pl.BlockSpec(memory_space=pltpu.SMEM)


def dot_nn(left, right):
    return jnp.dot(left, right, preferred_element_type=F32)


def dot_nt(left, right):
    return lax.dot_general(left, right, (((1,), (1,)), ((), ())), preferred_element_type=F32)


def dot_tn(left, right):
    return lax.dot_general(left, right, (((0,), (0,)), ((), ())), preferred_element_type=F32)


def swap_cores(array):
    size = lax.axis_size("dp")
    return lax.ppermute(array, "dp", [(i, i ^ 1) for i in range(size)])


def next_chip(array, sign):
    size = lax.axis_size("dp")
    return lax.ppermute(array, "dp", [(i, (i + 2 * sign) % size) for i in range(size)])


def f32_sum(*terms):
    total = terms[0].astype(F32)
    for term in terms[1:]:
        total = total + term.astype(F32)
    return total.astype(BF16)


def chunk_of(pre_ref, down_ref):
    return jnp.concatenate([pre_ref[...], down_ref[...]], axis=1)


def split_kernel(pre_ref, down_ref, front_out, back_out):
    half = front_out.shape[0]
    edge = pre_ref.shape[1]
    for out, rows in ((front_out, slice(0, half)), (back_out, slice(half, 2 * half))):
        out[:, :edge] = pre_ref[rows, :]
        out[:, edge:] = down_ref[rows, :]


def join_kernel(forward_ref, backward_ref, pre_front, down_front, pre_back, down_back, front_out, back_out):
    half = forward_ref.shape[0]
    front, back = chunk_of(pre_front, down_front), chunk_of(pre_back, down_back)
    front_out[:half] = f32_sum(forward_ref[...], front[:half])
    front_out[half:] = front[half:]
    back_out[:half] = back[:half]
    back_out[half:] = f32_sum(backward_ref[...], back[half:])


def add_kernel(forward_ref, backward_ref, pre_front, down_front, pre_back, down_back, front_out, back_out):
    front_out[...] = f32_sum(forward_ref[...], chunk_of(pre_front, down_front))
    back_out[...] = f32_sum(backward_ref[...], chunk_of(pre_back, down_back))


def finish_kernel(forward_ref, backward_ref, pre_ref, down_ref, gate_out, up_out, down_out):
    forward, backward = forward_ref[...], backward_ref[...]
    if forward.shape != gate_out.shape[1:2] + forward.shape[1:]:
        arrived = jnp.concatenate([forward, backward], axis=0).astype(F32)
    else:
        arrived = forward.astype(F32) + backward.astype(F32)
    total = chunk_of(pre_ref, down_ref).astype(F32) + arrived
    hidden = gate_out.shape[2]
    gate_out[0] = total[:, :hidden].astype(BF16)
    up_out[0] = total[:, hidden : 2 * hidden].astype(BF16)
    down_out[0] = total[:, 2 * hidden :].T.astype(BF16)


class Sums:
    def __init__(self, far, parts, block, chips):
        self.parts, self.block, self.chips = parts, block, chips
        self.widths = [part.shape[1] for part in parts]
        self.distance = chips // 2
        half = jax.ShapeDtypeStruct((block // 2, sum(self.widths)), BF16)
        self.operands = call(split_kernel, (half, half), [VMEM, VMEM], far, 8, 1, 1)
        self.send(self.operands)

    def specs(self, away):
        place = away % self.chips
        return [pl.BlockSpec((self.block, width), lambda step: (place, 0)) for width in self.widths]

    def send(self, operands):
        self.moving = (next_chip(operands[0], 1), next_chip(operands[1], -1))

    def step(self):
        kernel = join_kernel if self.distance == self.chips // 2 else add_kernel
        self.distance -= 1
        out = jax.ShapeDtypeStruct((self.block, sum(self.widths)), BF16)
        return call(
            kernel,
            (out, out),
            [VMEM, VMEM, *self.specs(self.distance), *self.specs(-self.distance)],
            (*self.moving, *self.parts, *self.parts),
            12, 1, 1, (1,),
        )

    def finish(self, out_shapes, after):
        arrived, _ = lax.optimization_barrier((self.moving, after))
        return call(
            finish_kernel,
            out_shapes,
            [VMEM, VMEM, *self.specs(0)],
            (*arrived, *self.parts),
            12, 1, 1, (1,),
        )


def select_matrix(most, tok_dev, base_ref, picks_ref):
    local = picks_ref[...] - base_ref[0]
    experts, slots = local.shape
    below = jnp.sum((local < 0).astype(F32), axis=1, keepdims=True).astype(I32)
    counter = lax.broadcasted_iota(I32, (most, 1), 0)
    spread = jnp.concatenate(
        [jnp.broadcast_to(local[e : e + 1], (most, slots)) for e in range(experts)], axis=0
    )
    wanted = jnp.concatenate([below[e : e + 1] + counter for e in range(experts)], axis=0)
    position = lax.broadcasted_iota(I32, spread.shape, 1)
    hit = (position == wanted) & (spread >= 0) & (spread < tok_dev)
    token = jnp.sum(jnp.where(hit, spread + 1, 0).astype(F32), axis=1, keepdims=True) - 1.0
    token_range = lax.broadcasted_iota(I32, (spread.shape[0], tok_dev), 1).astype(F32)
    return (token_range == token).astype(F32)


def send_kernel(most, base_ref, picks_ref, tokens_ref, cotangent_ref, out_ref):
    tok_dev, width = tokens_ref.shape
    select = select_matrix(most, tok_dev, base_ref, picks_ref).astype(BF16)
    out_ref[:, :width] = dot_nn(select, tokens_ref[...]).astype(BF16)
    out_ref[:, width:] = dot_nn(select, cotangent_ref[...]).astype(BF16)


def collect_matrix_kernel(most, base_ref, picks_ref, out_ref):
    out_ref[...] = select_matrix(most, out_ref.shape[0], base_ref, picks_ref).T.astype(BF16)


def gather_kernel(select_ref, tokens_ref, out_ref):
    out_ref[...] = dot_nn(select_ref[...], tokens_ref[...]).astype(BF16)


def take_kernel(most, tok_dev, own_ref, take_ref, turned_ref):
    slots, columns = take_ref.shape
    lane = lax.broadcasted_iota(I32, (1, columns), 1)
    source = jnp.zeros((1, columns), I32)
    for edge in range(most, columns, most):
        source = source + (lane >= edge).astype(I32)
    within = lane - source * most
    own = own_ref[...]
    start = jnp.sum((own < source * tok_dev).astype(F32), axis=0, keepdims=True)
    stop = jnp.sum((own < (source + 1) * tok_dev).astype(F32), axis=0, keepdims=True)
    slot = start + within.astype(F32)
    slot = jnp.where(slot < stop, slot, -1.0)
    slot_range = lax.broadcasted_iota(I32, (slots, columns), 0).astype(F32)
    hot = (slot_range == slot).astype(F32)
    take_ref[...] = hot.astype(BF16)
    turned_ref[...] = hot.T.astype(BF16)


def compact_kernel(
    chips, place_ref, take_ref, arrived_ref, scale_ref,
    rows_ref, rows_keep, rows_give, grads_ref, scaled_keep, scaled_give,
):
    chip, core = place_ref[0], place_ref[1]
    width = rows_ref.shape[1]
    block = width // (2 * chips)
    for k in range(chips):
        columns = slice(2 * k * block, 2 * (k + 1) * block)
        where = pl.ds(pl.multiple_of(lax.rem(k - chip + chips, chips) * block, block), block)
        rows = dot_nn(take_ref[...], arrived_ref[:, columns])
        behind = slice(width + 2 * k * block, width + 2 * (k + 1) * block)
        grads = dot_nn(take_ref[...], arrived_ref[:, behind])
        rows_ref[:, columns] = rows.astype(BF16)
        grads_ref[:, columns] = grads.astype(BF16)
        for value, keep_ref, give_ref in (
            (rows, rows_keep, rows_give), (grads * scale_ref[...], scaled_keep, scaled_give)
        ):
            even, odd = value[:, :block], value[:, block:]
            keep_ref[:, where] = jnp.where(core == 0, even, odd).astype(BF16)
            give_ref[:, where] = jnp.where(core == 0, odd, even).astype(BF16)


def expert_kernel(
    rows_ref, grads_ref, scale_ref, gate_ref, up_ref, down_ref, gate_grad, up_grad, hidden_ref, slot_ref
):
    @pl.when(pl.program_id(0) == 0)
    def _():
        slot_ref[...] = jnp.zeros(slot_ref.shape, F32)

    gate_pre = dot_nn(rows_ref[...], gate_ref[...])
    up_pre = dot_nn(rows_ref[...], up_ref[...])
    raw = dot_nt(grads_ref[...], down_ref[...])
    sigmoid_gate = jax.nn.sigmoid(gate_pre)
    activated = gate_pre * sigmoid_gate
    hidden = (activated * up_pre).astype(BF16)
    hidden_ref[...] = hidden
    slot_ref[...] += jnp.sum(raw * hidden.astype(F32), axis=1, keepdims=True)
    scaled = raw * scale_ref[...]
    slope = up_pre * sigmoid_gate * (1.0 + gate_pre * (1.0 - sigmoid_gate))
    gate_grad[...] = (scaled * slope).astype(BF16)
    up_grad[...] = (scaled * activated).astype(BF16)


def return_kernel(gate_grad, up_grad, turned_ref, gate_ref, up_ref, out_ref):
    row_grads = dot_nt(gate_grad[...], gate_ref[...]) + dot_nt(up_grad[...], up_ref[...])
    out_ref[...] = dot_nn(turned_ref[...], row_grads.astype(BF16)).astype(BF16)


def call(
    kernel, out_shapes, in_specs, operands, limit_mib, flops, bytes_accessed, grid=(), out_specs=None
):
    if out_specs is None:
        out_specs = jax.tree.map(lambda _: VMEM, out_shapes)
    return pl.pallas_call(
        kernel,
        grid=grid,
        out_shape=out_shapes,
        in_specs=in_specs,
        out_specs=out_specs,
        compiler_params=pltpu.CompilerParams(vmem_limit_bytes=limit_mib * 2**20),
        cost_estimate=pl.CostEstimate(
            flops=flops, bytes_accessed=bytes_accessed, transcendentals=0
        ),
    )(*operands)


def body(tokens, cotangent, picks, gates, w_gate, w_up, w_down):
    node_count = lax.axis_size("expert")
    self_index = lax.axis_index("expert")
    dp_size = lax.axis_size("dp")
    dp_index = lax.axis_index("dp")
    chips = dp_size // 2
    place = jnp.stack([lax.shift_right_logical(dp_index, 1), dp_index & 1]).astype(I32)
    tok_dev, width = tokens.shape
    slot_count = gates.shape[2]
    most = max(2, 3 * slot_count // (2 * node_count))
    padded = node_count * most
    hidden_width = w_gate.shape[2]
    block = width // dp_size

    def shape(*dims, dtype=BF16):
        return jax.ShapeDtypeStruct(dims, dtype)

    table = picks[0]
    base = (self_index * tok_dev).astype(I32).reshape(1)
    gate_rows = gates.reshape(slot_count, 1)
    outgoing = call(
        functools.partial(send_kernel, most),
        shape(padded, 2 * width),
        [SMEM, VMEM, VMEM, VMEM],
        (base, table, tokens, cotangent),
        12, 4 * padded * tok_dev * width, 8 * padded * width,
    )

    def exchange(array):
        shaped = array.reshape(node_count, most, array.shape[1])
        return lax.all_to_all(shaped, "expert", 0, 0, tiled=True).reshape(array.shape)

    arrived = exchange(outgoing)

    own = lax.dynamic_index_in_dim(table, self_index, 0, keepdims=False)
    take, take_turned = call(
        functools.partial(take_kernel, most, tok_dev),
        (shape(slot_count, padded), shape(padded, slot_count)),
        [VMEM],
        (own.reshape(slot_count, 1),),
        8, 8 * slot_count * padded, 2 * slot_count * padded,
    )
    select_turned = call(
        functools.partial(collect_matrix_kernel, most),
        shape(tok_dev, padded),
        [SMEM, VMEM],
        (base, table),
        8, 8 * slot_count * padded, 2 * slot_count * padded,
    )
    whole, part = shape(slot_count, width), shape(slot_count, width // 2)
    rows, rows_keep, rows_give, grads, scaled_keep, scaled_give = call(
        functools.partial(compact_kernel, chips),
        (whole, part, part, whole, part, part),
        [SMEM, VMEM, VMEM, VMEM],
        (place, take, arrived, gate_rows),
        16, 4 * slot_count * padded * width, 16 * slot_count * width,
    )
    tile = min(256, hidden_width)
    narrow = shape(slot_count, hidden_width)
    across = pl.BlockSpec((width, tile), lambda step: (0, step))
    result = pl.BlockSpec((slot_count, tile), lambda step: (0, step))
    gate_pre_grad, up_pre_grad, hidden, slot_grads = call(
        expert_kernel,
        (narrow, narrow, narrow, shape(slot_count, 1, dtype=F32)),
        [VMEM, VMEM, VMEM, across, across, pl.BlockSpec((tile, width), lambda step: (step, 0))],
        (rows, grads, gate_rows, w_gate[0], w_up[0], w_down[0]),
        52, 6 * slot_count * width * hidden_width, 6 * width * hidden_width,
        (hidden_width // tile,),
        (result, result, result, VMEM),
    )
    pre_grads = jnp.concatenate([gate_pre_grad, up_pre_grad], axis=1)
    rows_both = jnp.concatenate([rows_keep, swap_cores(rows_give)], axis=0)
    scaled_both = jnp.concatenate([scaled_keep, swap_cores(scaled_give)], axis=0)
    hidden_both = jnp.concatenate([hidden, swap_cores(hidden)], axis=0)
    pre_both = jnp.concatenate([pre_grads, swap_cores(pre_grads)], axis=0)

    def parts_of(columns):
        return (
            dot_tn(rows_both[:, columns], pre_both).astype(BF16),
            dot_tn(scaled_both[:, columns], hidden_both).astype(BF16),
        )

    row_tile = min(256, width)
    wide = pl.BlockSpec((row_tile, hidden_width), lambda step: (step, 0))

    def give_back(gate_pre_grad, up_pre_grad):
        return call(
            return_kernel,
            shape(padded, width),
            [VMEM, VMEM, VMEM, wide, wide],
            (gate_pre_grad, up_pre_grad, take_turned, w_gate[0], w_up[0]),
            12, 4 * slot_count * width * hidden_width, 4 * width * hidden_width,
            (width // row_tile,),
            pl.BlockSpec((padded, row_tile), lambda step: (0, step)),
        )

    def collect(came_back):
        return call(
            gather_kernel,
            shape(tok_dev, width),
            [VMEM, VMEM],
            (select_turned, came_back),
            12, 2 * padded * tok_dev * width, 4 * padded * width,
        )

    if chips > 1:
        farthest = chips // 2
        far = parts_of(slice(farthest * block, (farthest + 1) * block))
        parts = parts_of(slice(None))
        sums = Sums(far, parts, block, chips)
        held, _ = lax.optimization_barrier(((gate_pre_grad, up_pre_grad), sums.operands))
        returning = give_back(*held)
        sums.moving, returning = lax.optimization_barrier((sums.moving, returning))
        returned = None
        while sums.distance > 1:
            operands = sums.step()
            if returned is None:
                returning, _ = lax.optimization_barrier((returning, operands))
                returned = exchange(returning)
            sums.send(operands)
            latest = operands
        if returned is None:
            returned, latest = exchange(returning), returning
        returned, _ = lax.optimization_barrier((returned, latest))
        token_grads = collect(returned)
        weight_shapes = (
            shape(1, block, hidden_width),
            shape(1, block, hidden_width),
            shape(1, hidden_width, block),
        )
        weight_grads = sums.finish(weight_shapes, token_grads)
    else:
        token_grads = collect(exchange(give_back(gate_pre_grad, up_pre_grad)))
        pre_part, down_part = parts_of(slice(None))
        weight_grads = (*(half[None] for half in jnp.split(pre_part, 2, axis=1)), down_part.T[None])
    return (token_grads, slot_grads.reshape(1, 1, slot_count), *weight_grads)


def solution(mesh):
    return jax.shard_map(
        body,
        mesh=mesh,
        in_specs=(
            P(("dp", "expert"), None),
            P(("dp", "expert"), None),
            P("dp", None, None),
            P("dp", "expert", None),
            P("expert", None, None),
            P("expert", None, None),
            P("expert", None, None),
        ),
        out_specs=(
            P(("dp", "expert"), None),
            P("dp", "expert", None),
            P("expert", "dp", None),
            P("expert", "dp", None),
            P("expert", None, "dp"),
        ),
        check_vma=False,
    )
```

```python
import functools

import jax
import jax.numpy as jnp
from jax import lax
from jax.experimental import pallas as pl
from jax.experimental.pallas import tpu as pltpu
from jax.sharding import PartitionSpec as P

BF16 = jnp.bfloat16
F32 = jnp.float32
I32 = jnp.int32
VMEM = pl.BlockSpec(memory_space=pltpu.VMEM)
SMEM = pl.BlockSpec(memory_space=pltpu.SMEM)


def dot_nn(left, right):
    return jnp.dot(left, right, preferred_element_type=F32)


def dot_nt(left, right):
    return lax.dot_general(left, right, (((1,), (1,)), ((), ())), preferred_element_type=F32)


def dot_tn(left, right):
    return lax.dot_general(left, right, (((0,), (0,)), ((), ())), preferred_element_type=F32)


def swap_cores(array):
    size = lax.axis_size("dp")
    return lax.ppermute(array, "dp", [(i, i ^ 1) for i in range(size)])


def next_chip(array, sign):
    size = lax.axis_size("dp")
    return lax.ppermute(array, "dp", [(i, (i + 2 * sign) % size) for i in range(size)])


def f32_sum(*terms):
    total = terms[0].astype(F32)
    for term in terms[1:]:
        total = total + term.astype(F32)
    return total.astype(BF16)


def chunk_of(pre_ref, down_ref):
    return jnp.concatenate([pre_ref[...], down_ref[...]], axis=1)


def split_kernel(pre_ref, down_ref, front_out, back_out):
    half = front_out.shape[0]
    edge = pre_ref.shape[1]
    for out, rows in ((front_out, slice(0, half)), (back_out, slice(half, 2 * half))):
        out[:, :edge] = pre_ref[rows, :]
        out[:, edge:] = down_ref[rows, :]


def join_kernel(forward_ref, backward_ref, pre_front, down_front, pre_back, down_back, front_out, back_out):
    half = forward_ref.shape[0]
    front, back = chunk_of(pre_front, down_front), chunk_of(pre_back, down_back)
    front_out[:half] = f32_sum(forward_ref[...], front[:half])
    front_out[half:] = front[half:]
    back_out[:half] = back[:half]
    back_out[half:] = f32_sum(backward_ref[...], back[half:])


def add_kernel(forward_ref, backward_ref, pre_front, down_front, pre_back, down_back, front_out, back_out):
    front_out[...] = f32_sum(forward_ref[...], chunk_of(pre_front, down_front))
    back_out[...] = f32_sum(backward_ref[...], chunk_of(pre_back, down_back))


def finish_kernel(forward_ref, backward_ref, pre_ref, down_ref, gate_out, up_out, down_out):
    forward, backward = forward_ref[...], backward_ref[...]
    if forward.shape != gate_out.shape[1:2] + forward.shape[1:]:
        arrived = jnp.concatenate([forward, backward], axis=0).astype(F32)
    else:
        arrived = forward.astype(F32) + backward.astype(F32)
    total = chunk_of(pre_ref, down_ref).astype(F32) + arrived
    hidden = gate_out.shape[2]
    gate_out[0] = total[:, :hidden].astype(BF16)
    up_out[0] = total[:, hidden : 2 * hidden].astype(BF16)
    down_out[0] = total[:, 2 * hidden :].T.astype(BF16)


class Sums:
    def __init__(self, far, parts, block, chips):
        self.parts, self.block, self.chips = parts, block, chips
        self.widths = [part.shape[1] for part in parts]
        self.distance = chips // 2
        half = jax.ShapeDtypeStruct((block // 2, sum(self.widths)), BF16)
        self.send(call(split_kernel, (half, half), [VMEM, VMEM], far, 8, 1, 1))

    def specs(self, away):
        place = away % self.chips
        return [pl.BlockSpec((self.block, width), lambda step: (place, 0)) for width in self.widths]

    def send(self, operands):
        self.moving = (next_chip(operands[0], 1), next_chip(operands[1], -1))

    def step(self):
        kernel = join_kernel if self.distance == self.chips // 2 else add_kernel
        self.distance -= 1
        out = jax.ShapeDtypeStruct((self.block, sum(self.widths)), BF16)
        return call(
            kernel,
            (out, out),
            [VMEM, VMEM, *self.specs(self.distance), *self.specs(-self.distance)],
            (*self.moving, *self.parts, *self.parts),
            40, 1, 1, (1,),
        )

    def finish(self, out_shapes, after):
        arrived, _ = lax.optimization_barrier((self.moving, after))
        return call(
            finish_kernel,
            out_shapes,
            [VMEM, VMEM, *self.specs(0)],
            (*arrived, *self.parts),
            40, 1, 1, (1,),
        )


def select_matrix(most, tok_dev, base_ref, picks_ref):
    local = picks_ref[...] - base_ref[0]
    experts, slots = local.shape
    below = jnp.sum((local < 0).astype(F32), axis=1, keepdims=True).astype(I32)
    counter = lax.broadcasted_iota(I32, (most, 1), 0)
    spread = jnp.concatenate(
        [jnp.broadcast_to(local[e : e + 1], (most, slots)) for e in range(experts)], axis=0
    )
    wanted = jnp.concatenate([below[e : e + 1] + counter for e in range(experts)], axis=0)
    position = lax.broadcasted_iota(I32, spread.shape, 1)
    hit = (position == wanted) & (spread >= 0) & (spread < tok_dev)
    token = jnp.sum(jnp.where(hit, spread + 1, 0).astype(F32), axis=1, keepdims=True) - 1.0
    token_range = lax.broadcasted_iota(I32, (spread.shape[0], tok_dev), 1).astype(F32)
    return (token_range == token).astype(F32)


def select_kernel(most, base_ref, picks_ref, tokens_ref, select_ref, out_ref):
    select = select_matrix(most, tokens_ref.shape[0], base_ref, picks_ref).astype(BF16)
    select_ref[...] = select
    out_ref[...] = dot_nn(select, tokens_ref[...]).astype(BF16)


def collect_matrix_kernel(most, base_ref, picks_ref, out_ref):
    out_ref[...] = select_matrix(most, out_ref.shape[0], base_ref, picks_ref).T.astype(BF16)


def gather_kernel(select_ref, tokens_ref, out_ref):
    out_ref[...] = dot_nn(select_ref[...], tokens_ref[...]).astype(BF16)


def take_kernel(most, tok_dev, own_ref, take_ref, turned_ref):
    slots, columns = take_ref.shape
    lane = lax.broadcasted_iota(I32, (1, columns), 1)
    source = jnp.zeros((1, columns), I32)
    for edge in range(most, columns, most):
        source = source + (lane >= edge).astype(I32)
    within = lane - source * most
    own = own_ref[...]
    start = jnp.sum((own < source * tok_dev).astype(F32), axis=0, keepdims=True)
    stop = jnp.sum((own < (source + 1) * tok_dev).astype(F32), axis=0, keepdims=True)
    slot = start + within.astype(F32)
    slot = jnp.where(slot < stop, slot, -1.0)
    slot_range = lax.broadcasted_iota(I32, (slots, columns), 0).astype(F32)
    hot = (slot_range == slot).astype(F32)
    take_ref[...] = hot.astype(BF16)
    turned_ref[...] = hot.T.astype(BF16)


def compact_kernel(chips, place_ref, take_ref, arrived_ref, scale_ref, full_ref, keep_ref, give_ref):
    chip, core = place_ref[0], place_ref[1]
    block = arrived_ref.shape[1] // (2 * chips)
    for k in range(chips):
        columns = slice(2 * k * block, 2 * (k + 1) * block)
        value = dot_nn(take_ref[...], arrived_ref[:, columns])
        full_ref[:, columns] = value.astype(BF16)
        if scale_ref is not None:
            value = value * scale_ref[...]
        even, odd = value[:, :block], value[:, block:]
        where = pl.ds(pl.multiple_of(lax.rem(k - chip + chips, chips) * block, block), block)

        keep_ref[:, where] = jnp.where(core == 0, even, odd).astype(BF16)
        give_ref[:, where] = jnp.where(core == 0, odd, even).astype(BF16)


def plain_compact_kernel(chips, place_ref, take_ref, arrived_ref, full_ref, keep_ref, give_ref):
    compact_kernel(chips, place_ref, take_ref, arrived_ref, None, full_ref, keep_ref, give_ref)


def grad_kernel(
    tile, grads_ref, down_ref, gate_ref, hidden_ref, slope_ref, activated_ref, pre_ref, slot_ref
):
    hidden_width = down_ref.shape[0]
    total = jnp.zeros(slot_ref.shape, F32)
    for begin in range(0, hidden_width, tile):
        columns = slice(begin, begin + tile)
        raw = dot_nt(grads_ref[...], down_ref[columns, :])
        total = total + jnp.sum(raw * hidden_ref[:, columns].astype(F32), axis=1, keepdims=True)
        scaled = raw * gate_ref[...]
        pre_ref[:, columns] = (scaled * slope_ref[:, columns]).astype(BF16)
        other = slice(hidden_width + begin, hidden_width + begin + tile)
        pre_ref[:, other] = (scaled * activated_ref[:, columns]).astype(BF16)
    slot_ref[...] = total


def park_kernel(array_ref, out_ref):
    out_ref[...] = array_ref[...]


def return_kernel(tile, pre_ref, gate_ref, up_ref, turned_ref, out_ref, held):
    width, hidden_width = gate_ref.shape
    for begin in range(0, width, tile):
        columns = slice(begin, begin + tile)
        row_grads = dot_nt(pre_ref[:, :hidden_width], gate_ref[columns, :]) + dot_nt(
            pre_ref[:, hidden_width:], up_ref[columns, :]
        )
        held[:, columns] = row_grads.astype(BF16)
    for begin in range(0, width, 2 * tile):
        columns = slice(begin, begin + 2 * tile)
        out_ref[:, columns] = dot_nn(turned_ref[...], held[:, columns]).astype(BF16)


def call(kernel, out_shapes, in_specs, operands, limit_mib, flops, bytes_accessed, grid=(), scratch=()):
    return pl.pallas_call(
        kernel,
        grid=grid,
        out_shape=out_shapes,
        in_specs=in_specs,
        out_specs=jax.tree.map(lambda _: VMEM, out_shapes),
        scratch_shapes=scratch,
        compiler_params=pltpu.CompilerParams(vmem_limit_bytes=limit_mib * 2**20),
        cost_estimate=pl.CostEstimate(
            flops=flops, bytes_accessed=bytes_accessed, transcendentals=0
        ),
    )(*operands)


def body(tokens, cotangent, picks, gates, w_gate, w_up, w_down):
    node_count = lax.axis_size("expert")
    self_index = lax.axis_index("expert")
    dp_size = lax.axis_size("dp")
    dp_index = lax.axis_index("dp")
    chips = dp_size // 2
    place = jnp.stack([lax.shift_right_logical(dp_index, 1), dp_index & 1]).astype(I32)
    tok_dev, width = tokens.shape
    slot_count = gates.shape[2]
    most = max(2, 3 * slot_count // (2 * node_count))
    padded = node_count * most
    hidden_width = w_gate.shape[2]
    block = width // dp_size

    def shape(*dims, dtype=BF16):
        return jax.ShapeDtypeStruct(dims, dtype)

    table = picks[0]
    base = (self_index * tok_dev).astype(I32).reshape(1)
    select, out_rows = call(
        lambda *refs: select_kernel(most, *refs),
        (shape(padded, tok_dev), shape(padded, width)),
        [SMEM, VMEM, VMEM],
        (base, table, tokens),
        16, 2 * padded * tok_dev * width, 4 * padded * width,
    )
    out_grads = call(
        gather_kernel,
        shape(padded, width),
        [VMEM, VMEM],
        (select, cotangent),
        16, 2 * padded * tok_dev * width, 4 * padded * width,
    )

    def exchange(array):
        shaped = array.reshape(node_count, most, width)
        return lax.all_to_all(shaped, "expert", 0, 0, tiled=True).reshape(padded, width)

    arrived_rows = exchange(out_rows)
    arrived_grads = exchange(out_grads)

    own = lax.dynamic_index_in_dim(table, self_index, 0, keepdims=False)
    take, take_turned = call(
        lambda *refs: take_kernel(most, tok_dev, *refs),
        (shape(slot_count, padded), shape(padded, slot_count)),
        [VMEM],
        (own.reshape(slot_count, 1),),
        8, 8 * slot_count * padded, 2 * slot_count * padded,
    )
    select_turned = call(
        functools.partial(collect_matrix_kernel, most),
        shape(tok_dev, padded),
        [SMEM, VMEM],
        (base, table),
        8, 8 * slot_count * padded, 2 * slot_count * padded,
    )
    compact_shapes = (
        shape(slot_count, width), shape(slot_count, width // 2), shape(slot_count, width // 2)
    )
    compact_cost = (12, 2 * slot_count * padded * width, 8 * slot_count * width)
    rows, rows_keep, rows_give = call(
        lambda *refs: plain_compact_kernel(chips, *refs),
        compact_shapes,
        [SMEM, VMEM, VMEM],
        (place, take, arrived_rows),
        *compact_cost,
    )
    rows_both = jnp.concatenate([rows_keep, swap_cores(rows_give)], axis=0)
    gate_pre = dot_nn(rows, w_gate[0])
    up_pre = dot_nn(rows, w_up[0])
    sigmoid_gate = jax.nn.sigmoid(gate_pre)
    activated = gate_pre * sigmoid_gate
    slope = up_pre * sigmoid_gate * (1.0 + gate_pre * (1.0 - sigmoid_gate))
    hidden = (activated * up_pre).astype(BF16)
    hidden_both = jnp.concatenate([hidden, swap_cores(hidden)], axis=0)

    gate_rows = gates.reshape(slot_count, 1)
    down_weight = call(
        park_kernel,
        shape(hidden_width, width),
        [VMEM],
        (w_down[0],),
        8, 1, 4 * width * hidden_width,
    )
    arrived_grads, hidden, slope, activated, rows_both, hidden_both, down_weight = (
        lax.optimization_barrier(
            (arrived_grads, hidden, slope, activated, rows_both, hidden_both, down_weight)
        )
    )
    grads, scaled_keep, scaled_give = call(
        lambda *refs: compact_kernel(chips, *refs),
        compact_shapes,
        [SMEM, VMEM, VMEM, VMEM],
        (place, take, arrived_grads, gate_rows),
        *compact_cost,
    )
    scaled_both = jnp.concatenate([scaled_keep, swap_cores(scaled_give)], axis=0)
    pre_grads, slot_grads = call(
        lambda *refs: grad_kernel(min(256, hidden_width), *refs),
        (shape(slot_count, 2 * hidden_width), shape(slot_count, 1, dtype=F32)),
        [VMEM] * 6,
        (grads, down_weight, gate_rows, hidden, slope, activated),
        16, 2 * slot_count * width * hidden_width, 2 * width * hidden_width,
    )
    pre_both = jnp.concatenate([pre_grads, swap_cores(pre_grads)], axis=0)

    def parts_of(columns):
        return (
            dot_tn(rows_both[:, columns], pre_both).astype(BF16),
            dot_tn(scaled_both[:, columns], hidden_both).astype(BF16),
        )

    def give_back(pre_grads):
        return call(
            functools.partial(return_kernel, min(256, width)),
            shape(padded, width),
            [VMEM] * 4,
            (pre_grads, w_gate[0], w_up[0], take_turned),
            16, 4 * slot_count * width * hidden_width, 4 * width * hidden_width,
            scratch=(pltpu.VMEM((slot_count, width), BF16),),
        )

    def collect(came_back):
        return call(
            gather_kernel,
            shape(tok_dev, width),
            [VMEM, VMEM],
            (select_turned, came_back),
            12, 2 * padded * tok_dev * width, 4 * padded * width,
        )

    if chips > 1:
        farthest = chips // 2
        far = parts_of(slice(farthest * block, (farthest + 1) * block))
        parts = parts_of(slice(None))
        sums = Sums(far, parts, block, chips)
        returning = give_back(pre_grads)
        returned = None
        while sums.distance > 1:
            operands = sums.step()
            if returned is None:
                returning, _ = lax.optimization_barrier((returning, operands))
                returned = exchange(returning)
            sums.send(operands)
            latest = operands
        if returned is None:
            returned, latest = exchange(returning), returning
        returned, _ = lax.optimization_barrier((returned, latest))
        token_grads = collect(returned)
        weight_shapes = (
            shape(1, block, hidden_width),
            shape(1, block, hidden_width),
            shape(1, hidden_width, block),
        )
        weight_grads = sums.finish(weight_shapes, token_grads)
    else:
        token_grads = collect(exchange(give_back(pre_grads)))
        pre_part, down_part = parts_of(slice(None))
        weight_grads = (*(half[None] for half in jnp.split(pre_part, 2, axis=1)), down_part.T[None])
    return (token_grads, slot_grads.reshape(1, 1, slot_count), *weight_grads)


def solution(mesh):
    return jax.shard_map(
        body,
        mesh=mesh,
        in_specs=(
            P(("dp", "expert"), None),
            P(("dp", "expert"), None),
            P("dp", None, None),
            P("dp", "expert", None),
            P("expert", None, None),
            P("expert", None, None),
            P("expert", None, None),
        ),
        out_specs=(
            P(("dp", "expert"), None),
            P("dp", "expert", None),
            P("expert", "dp", None),
            P("expert", "dp", None),
            P("expert", None, "dp"),
        ),
        check_vma=False,
    )
```

```python
import functools

import jax
import jax.numpy as jnp
from jax import lax
from jax.experimental import pallas as pl
from jax.experimental.pallas import tpu as pltpu
from jax.sharding import PartitionSpec as P

BF16 = jnp.bfloat16
F32 = jnp.float32
I32 = jnp.int32
VMEM = pl.BlockSpec(memory_space=pltpu.VMEM)
SMEM = pl.BlockSpec(memory_space=pltpu.SMEM)


def dot_nn(left, right):
    return jnp.dot(left, right, preferred_element_type=F32)


def dot_nt(left, right):
    return lax.dot_general(left, right, (((1,), (1,)), ((), ())), preferred_element_type=F32)


def dot_tn(left, right):
    return lax.dot_general(left, right, (((0,), (0,)), ((), ())), preferred_element_type=F32)


def swap_cores(array):
    size = lax.axis_size("dp")
    return lax.ppermute(array, "dp", [(i, i ^ 1) for i in range(size)])


def next_chip(array, sign):
    size = lax.axis_size("dp")
    return lax.ppermute(array, "dp", [(i, (i + 2 * sign) % size) for i in range(size)])


def f32_sum(*terms):
    total = terms[0].astype(F32)
    for term in terms[1:]:
        total = total + term.astype(F32)
    return total.astype(BF16)


def chunk_of(pre_ref, down_ref):
    return jnp.concatenate([pre_ref[...], down_ref[...]], axis=1)


def far_kernel(
    rows_own, rows_got, scaled_own, scaled_got, pre_own, pre_got, hidden_own, hidden_got,
    front_out, back_out,
):
    half = front_out.shape[0]
    edge = pre_own.shape[1]
    pre = dot_tn(rows_own[...], pre_own[...]) + dot_tn(rows_got[...], pre_got[...])
    down = dot_tn(scaled_own[...], hidden_own[...]) + dot_tn(scaled_got[...], hidden_got[...])
    for out, rows in ((front_out, slice(0, half)), (back_out, slice(half, 2 * half))):
        out[:, :edge] = pre[rows].astype(BF16)
        out[:, edge:] = down[rows].astype(BF16)


def join_kernel(forward_ref, backward_ref, pre_front, down_front, pre_back, down_back, front_out, back_out):
    half = forward_ref.shape[0]
    front, back = chunk_of(pre_front, down_front), chunk_of(pre_back, down_back)
    front_out[:half] = f32_sum(forward_ref[...], front[:half])
    front_out[half:] = front[half:]
    back_out[:half] = back[:half]
    back_out[half:] = f32_sum(backward_ref[...], back[half:])


def add_kernel(forward_ref, backward_ref, pre_front, down_front, pre_back, down_back, front_out, back_out):
    front_out[...] = f32_sum(forward_ref[...], chunk_of(pre_front, down_front))
    back_out[...] = f32_sum(backward_ref[...], chunk_of(pre_back, down_back))


def finish_kernel(forward_ref, backward_ref, pre_ref, down_ref, gate_out, up_out, down_out):
    forward, backward = forward_ref[...], backward_ref[...]
    if forward.shape != gate_out.shape[1:2] + forward.shape[1:]:
        arrived = jnp.concatenate([forward, backward], axis=0).astype(F32)
    else:
        arrived = forward.astype(F32) + backward.astype(F32)
    total = chunk_of(pre_ref, down_ref).astype(F32) + arrived
    hidden = gate_out.shape[2]
    gate_out[0] = total[:, :hidden].astype(BF16)
    up_out[0] = total[:, hidden : 2 * hidden].astype(BF16)
    down_out[0] = total[:, 2 * hidden :].T.astype(BF16)


class Sums:
    def __init__(self, sides, widths, block, chips):
        self.block, self.chips, self.widths = block, chips, widths
        self.distance = chips // 2
        half = jax.ShapeDtypeStruct((block // 2, sum(widths)), BF16)
        slots = sides[0].shape[0]
        chunk = pl.BlockSpec((slots, block), lambda step: (0, chips // 2))
        whole = [pl.BlockSpec(side.shape, lambda step: (0, 0)) for side in sides[4:]]
        self.operands = call(
            far_kernel, (half, half), [chunk] * 4 + whole, sides,
            54, 4 * slots * block * sum(widths), 4 * slots * sum(widths), (1,),
        )
        self.send(self.operands)

    def specs(self, away):
        place = away % self.chips
        return [pl.BlockSpec((self.block, width), lambda step: (place, 0)) for width in self.widths]

    def send(self, operands):
        self.moving = (next_chip(operands[0], 1), next_chip(operands[1], -1))

    def step(self):
        kernel = join_kernel if self.distance == self.chips // 2 else add_kernel
        self.distance -= 1
        out = jax.ShapeDtypeStruct((self.block, sum(self.widths)), BF16)
        return call(
            kernel,
            (out, out),
            [VMEM, VMEM, *self.specs(self.distance), *self.specs(-self.distance)],
            (*self.moving, *self.parts, *self.parts),
            40, 1, 1, (1,),
        )

    def finish(self, out_shapes, after):
        arrived, _ = lax.optimization_barrier((self.moving, after))
        return call(
            finish_kernel,
            out_shapes,
            [VMEM, VMEM, *self.specs(0)],
            (*arrived, *self.parts),
            40, 1, 1, (1,),
        )


def select_matrix(most, tok_dev, base_ref, picks_ref):
    local = picks_ref[...] - base_ref[0]
    experts, slots = local.shape
    below = jnp.sum((local < 0).astype(F32), axis=1, keepdims=True).astype(I32)
    counter = lax.broadcasted_iota(I32, (most, 1), 0)
    spread = jnp.concatenate(
        [jnp.broadcast_to(local[e : e + 1], (most, slots)) for e in range(experts)], axis=0
    )
    wanted = jnp.concatenate([below[e : e + 1] + counter for e in range(experts)], axis=0)
    position = lax.broadcasted_iota(I32, spread.shape, 1)
    hit = (position == wanted) & (spread >= 0) & (spread < tok_dev)
    token = jnp.sum(jnp.where(hit, spread + 1, 0).astype(F32), axis=1, keepdims=True) - 1.0
    token_range = lax.broadcasted_iota(I32, (spread.shape[0], tok_dev), 1).astype(F32)
    return (token_range == token).astype(F32)


def select_kernel(most, base_ref, picks_ref, tokens_ref, select_ref, out_ref):
    select = select_matrix(most, tokens_ref.shape[0], base_ref, picks_ref).astype(BF16)
    select_ref[...] = select
    out_ref[...] = dot_nn(select, tokens_ref[...]).astype(BF16)


def collect_matrix_kernel(most, base_ref, picks_ref, out_ref):
    out_ref[...] = select_matrix(most, out_ref.shape[0], base_ref, picks_ref).T.astype(BF16)


def gather_kernel(select_ref, tokens_ref, out_ref):
    out_ref[...] = dot_nn(select_ref[...], tokens_ref[...]).astype(BF16)


def as_column(row):
    size = row.shape[1]
    same = lax.broadcasted_iota(I32, (size, size), 0) == lax.broadcasted_iota(I32, (size, size), 1)
    return jnp.sum(jnp.where(same, row, 0.0), axis=1, keepdims=True)


def take_kernel(most, tok_dev, picks_ref, gates_ref, take_ref, turned_ref, gate_ref):
    slots, columns = take_ref.shape
    lane = lax.broadcasted_iota(I32, (1, columns), 1)
    source = jnp.zeros((1, columns), I32)
    for edge in range(most, columns, most):
        source = source + (lane >= edge).astype(I32)
    within = lane - source * most
    bound = (source * tok_dev).astype(F32)
    own = as_column(picks_ref[pl.ds(lax.axis_index("expert"), 1), :].astype(F32))
    start = jnp.sum((own < bound).astype(F32), axis=0, keepdims=True)
    stop = jnp.sum((own < bound + tok_dev).astype(F32), axis=0, keepdims=True)
    slot = start + within.astype(F32)
    slot = jnp.where(slot < stop, slot, -1.0)
    slot_range = lax.broadcasted_iota(I32, (slots, columns), 0).astype(F32)
    hot = (slot_range == slot).astype(F32)
    take_ref[...] = hot.astype(BF16)
    turned_ref[...] = hot.T.astype(BF16)
    gate_ref[...] = as_column(gates_ref[...])


def compact_kernel(chips, take_ref, arrived_ref, scale_ref, full_ref, keep_ref, give_ref):
    dp_index = lax.axis_index("dp")
    chip, core = lax.shift_right_logical(dp_index, 1), dp_index & 1
    block = arrived_ref.shape[1] // (2 * chips)
    for k in range(chips):
        columns = slice(2 * k * block, 2 * (k + 1) * block)
        value = dot_nn(take_ref[...], arrived_ref[:, columns])
        full_ref[:, columns] = value.astype(BF16)
        if scale_ref is not None:
            value = value * scale_ref[...]
        even, odd = value[:, :block], value[:, block:]
        where = pl.ds(pl.multiple_of(lax.rem(k - chip + chips, chips) * block, block), block)

        keep_ref[:, where] = jnp.where(core == 0, even, odd).astype(BF16)
        give_ref[:, where] = jnp.where(core == 0, odd, even).astype(BF16)


def plain_compact_kernel(chips, take_ref, arrived_ref, full_ref, keep_ref, give_ref):
    compact_kernel(chips, take_ref, arrived_ref, None, full_ref, keep_ref, give_ref)


def grad_kernel(
    chips, tile, arrived_ref, take_hbm, gate_hbm, down_hbm, hidden_hbm, slope_hbm, activated_hbm,
    keep_ref, give_ref, pre_ref, slot_ref,
    take_ref, gate_ref, down_ref, hidden_ref, slope_ref, activated_ref, grads_ref, arrivals,
):
    sources = (take_hbm, gate_hbm, down_hbm, hidden_hbm, slope_hbm, activated_hbm)
    targets = (take_ref, gate_ref, down_ref, hidden_ref, slope_ref, activated_ref)
    copies = [
        pltpu.make_async_copy(source, target, arrivals.at[index])
        for index, (source, target) in enumerate(zip(sources, targets))
    ]
    for copy in copies:
        copy.start()
    copies[0].wait()
    copies[1].wait()
    compact_kernel(chips, take_ref, arrived_ref, gate_ref, grads_ref, keep_ref, give_ref)
    for copy in copies[2:]:
        copy.wait()
    hidden_width = down_ref.shape[0]
    total = jnp.zeros(slot_ref.shape, F32)
    for begin in range(0, hidden_width, tile):
        columns = slice(begin, begin + tile)
        raw = dot_nt(grads_ref[...], down_ref[columns, :])
        total = total + jnp.sum(raw * hidden_ref[:, columns].astype(F32), axis=1, keepdims=True)
        scaled = raw * gate_ref[...]
        pre_ref[:, columns] = (scaled * slope_ref[:, columns]).astype(BF16)
        other = slice(hidden_width + begin, hidden_width + begin + tile)
        pre_ref[:, other] = (scaled * activated_ref[:, columns]).astype(BF16)
    slot_ref[...] = total


def forward_kernel(tile, rows_ref, gate_ref, up_ref, hidden_ref, slope_ref, activated_ref):
    for begin in range(0, gate_ref.shape[1], tile):
        columns = slice(begin, begin + tile)
        gate_pre = dot_nn(rows_ref[...], gate_ref[:, columns])
        up_pre = dot_nn(rows_ref[...], up_ref[:, columns])
        sigmoid_gate = jax.nn.sigmoid(gate_pre)
        activated = gate_pre * sigmoid_gate
        hidden_ref[:, columns] = (activated * up_pre).astype(BF16)
        activated_ref[:, columns] = activated
        slope_ref[:, columns] = up_pre * sigmoid_gate * (1.0 + gate_pre * (1.0 - sigmoid_gate))


def return_kernel(tile, pre_ref, gate_ref, up_ref, turned_ref, out_ref, held):
    width, hidden_width = gate_ref.shape
    for begin in range(0, width, tile):
        columns = slice(begin, begin + tile)
        row_grads = dot_nt(pre_ref[:, :hidden_width], gate_ref[columns, :]) + dot_nt(
            pre_ref[:, hidden_width:], up_ref[columns, :]
        )
        held[:, columns] = row_grads.astype(BF16)
    for begin in range(0, width, 2 * tile):
        columns = slice(begin, begin + 2 * tile)
        out_ref[:, columns] = dot_nn(turned_ref[...], held[:, columns]).astype(BF16)


def call(kernel, out_shapes, in_specs, operands, limit_mib, flops, bytes_accessed, grid=(), scratch=()):
    return pl.pallas_call(
        kernel,
        grid=grid,
        out_shape=out_shapes,
        in_specs=in_specs,
        out_specs=jax.tree.map(lambda _: VMEM, out_shapes),
        scratch_shapes=scratch,
        compiler_params=pltpu.CompilerParams(vmem_limit_bytes=limit_mib * 2**20),
        cost_estimate=pl.CostEstimate(
            flops=flops, bytes_accessed=bytes_accessed, transcendentals=0
        ),
    )(*operands)


def body(tokens, cotangent, picks, gates, w_gate, w_up, w_down):
    node_count = lax.axis_size("expert")
    self_index = lax.axis_index("expert")
    dp_size = lax.axis_size("dp")
    dp_index = lax.axis_index("dp")
    chips = dp_size // 2
    tok_dev, width = tokens.shape
    slot_count = gates.shape[2]
    most = max(2, 3 * slot_count // (2 * node_count))
    padded = node_count * most
    hidden_width = w_gate.shape[2]
    block = width // dp_size

    def shape(*dims, dtype=BF16):
        return jax.ShapeDtypeStruct(dims, dtype)

    table = picks[0]
    base = (self_index * tok_dev).astype(I32).reshape(1)
    select, out_rows = call(
        lambda *refs: select_kernel(most, *refs),
        (shape(padded, tok_dev), shape(padded, width)),
        [SMEM, VMEM, VMEM],
        (base, table, tokens),
        16, 2 * padded * tok_dev * width, 4 * padded * width,
    )
    out_grads = call(
        gather_kernel,
        shape(padded, width),
        [VMEM, VMEM],
        (select, cotangent),
        16, 2 * padded * tok_dev * width, 4 * padded * width,
    )

    def exchange(array):
        shaped = array.reshape(node_count, most, width)
        return lax.all_to_all(shaped, "expert", 0, 0, tiled=True).reshape(padded, width)

    arrived_rows = exchange(out_rows)
    arrived_grads = exchange(out_grads)

    held_table, arrived_rows = lax.optimization_barrier((table, arrived_rows))
    take, take_turned, gate_rows = call(
        functools.partial(take_kernel, most, tok_dev),
        (shape(slot_count, padded), shape(padded, slot_count), shape(slot_count, 1, dtype=F32)),
        [VMEM, VMEM],
        (held_table, gates.reshape(1, slot_count)),
        8, 8 * slot_count * padded, 2 * slot_count * padded,
    )
    select_turned = call(
        functools.partial(collect_matrix_kernel, most),
        shape(tok_dev, padded),
        [SMEM, VMEM],
        (base, table),
        8, 8 * slot_count * padded, 2 * slot_count * padded,
    )
    compact_shapes = (
        shape(slot_count, width), shape(slot_count, width // 2), shape(slot_count, width // 2)
    )
    origin = lambda step: (0, 0)
    compact_cost = (12, 2 * slot_count * padded * width, 8 * slot_count * width)
    rows, rows_keep, rows_give = call(
        lambda *refs: plain_compact_kernel(chips, *refs),
        compact_shapes,
        [pl.BlockSpec(take.shape, origin), VMEM],
        (take, arrived_rows),
        *compact_cost,
        grid=(1,),
    )
    narrow = (slot_count, hidden_width)
    hidden, slope, activated = call(
        functools.partial(forward_kernel, min(256, hidden_width)),
        (shape(*narrow), shape(*narrow, dtype=F32), shape(*narrow, dtype=F32)),
        [VMEM] * 3,
        (rows, w_gate[0], w_up[0]),
        16, 4 * slot_count * width * hidden_width, 4 * width * hidden_width,
    )
    rows_got, hidden_got = swap_cores(rows_give), swap_cores(hidden)
    arrived_grads, hidden, slope, activated, rows_got, hidden_got = lax.optimization_barrier(
        (arrived_grads, hidden, slope, activated, rows_got, hidden_got)
    )
    operands = (take, gate_rows, w_down[0], hidden, slope, activated)
    scaled_keep, scaled_give, pre_grads, slot_grads = call(
        functools.partial(grad_kernel, chips, min(256, hidden_width)),
        (
            shape(slot_count, width // 2),
            shape(slot_count, width // 2),
            shape(slot_count, 2 * hidden_width),
            shape(slot_count, 1, dtype=F32),
        ),
        [VMEM] + [pl.BlockSpec(memory_space=pl.ANY)] * 6,
        (arrived_grads, *operands),
        54,
        2 * slot_count * width * (padded + hidden_width),
        2 * width * hidden_width,
        scratch=(
            *(pltpu.VMEM(operand.shape, operand.dtype) for operand in operands),
            pltpu.VMEM((slot_count, width), BF16),
            pltpu.SemaphoreType.DMA((6,)),
        ),
    )
    scaled_got = swap_cores(scaled_give)
    pre_got = swap_cores(pre_grads)
    sides = (
        rows_keep, rows_got, scaled_keep, scaled_got, pre_grads, pre_got, hidden, hidden_got
    )

    def whole_parts(sides):
        pairs = [jnp.concatenate(sides[2 * k : 2 * k + 2], axis=0) for k in range(4)]
        return (
            dot_tn(pairs[0], pairs[2]).astype(BF16), dot_tn(pairs[1], pairs[3]).astype(BF16)
        )

    def give_back(pre_grads):
        return call(
            functools.partial(return_kernel, min(256, width)),
            shape(padded, width),
            [VMEM] * 4,
            (pre_grads, w_gate[0], w_up[0], take_turned),
            16, 4 * slot_count * width * hidden_width, 4 * width * hidden_width,
            scratch=(pltpu.VMEM((slot_count, width), BF16),),
        )

    def collect(came_back):
        return call(
            gather_kernel,
            shape(tok_dev, width),
            [VMEM, VMEM],
            (select_turned, came_back),
            12, 2 * padded * tok_dev * width, 4 * padded * width,
        )

    if chips > 1:
        sums = Sums(sides, [2 * hidden_width, hidden_width], block, chips)
        held_sides, _ = lax.optimization_barrier((sides, sums.operands))
        sums.parts = whole_parts(held_sides)
        returning = give_back(pre_grads)
        returned = None
        while sums.distance > 1:
            operands = sums.step()
            if returned is None:
                returning, _ = lax.optimization_barrier((returning, operands))
                returned = exchange(returning)
            sums.send(operands)
            latest = operands
        if returned is None:
            returned, latest = exchange(returning), returning
        returned, _ = lax.optimization_barrier((returned, latest))
        token_grads = collect(returned)
        weight_shapes = (
            shape(1, block, hidden_width),
            shape(1, block, hidden_width),
            shape(1, hidden_width, block),
        )
        weight_grads = sums.finish(weight_shapes, token_grads)
    else:
        token_grads = collect(exchange(give_back(pre_grads)))
        pre_part, down_part = whole_parts(sides)
        weight_grads = (*(half[None] for half in jnp.split(pre_part, 2, axis=1)), down_part.T[None])
    return (token_grads, slot_grads.reshape(1, 1, slot_count), *weight_grads)


def solution(mesh):
    return jax.shard_map(
        body,
        mesh=mesh,
        in_specs=(
            P(("dp", "expert"), None),
            P(("dp", "expert"), None),
            P("dp", None, None),
            P("dp", "expert", None),
            P("expert", None, None),
            P("expert", None, None),
            P("expert", None, None),
        ),
        out_specs=(
            P(("dp", "expert"), None),
            P("dp", "expert", None),
            P("expert", "dp", None),
            P("expert", "dp", None),
            P("expert", None, "dp"),
        ),
        check_vma=False,
    )
```

```python
import functools

import jax
import jax.numpy as jnp
from jax import lax
from jax.experimental import pallas as pl
from jax.experimental.pallas import tpu as pltpu
from jax.sharding import PartitionSpec as P

BF16 = jnp.bfloat16
F32 = jnp.float32
I32 = jnp.int32
VMEM = pl.BlockSpec(memory_space=pltpu.VMEM)
SMEM = pl.BlockSpec(memory_space=pltpu.SMEM)


def dot_nn(left, right):
    return jnp.dot(left, right, preferred_element_type=F32)


def dot_nt(left, right):
    return lax.dot_general(left, right, (((1,), (1,)), ((), ())), preferred_element_type=F32)


def dot_tn(left, right):
    return lax.dot_general(left, right, (((0,), (0,)), ((), ())), preferred_element_type=F32)


def swap_cores(array):
    size = lax.axis_size("dp")
    return lax.ppermute(array, "dp", [(i, i ^ 1) for i in range(size)])


def next_chip(array, sign):
    size = lax.axis_size("dp")
    return lax.ppermute(array, "dp", [(i, (i + 2 * sign) % size) for i in range(size)])


def f32_sum(*terms):
    total = terms[0].astype(F32)
    for term in terms[1:]:
        total = total + term.astype(F32)
    return total.astype(BF16)


def chunk_of(pre_ref, down_ref):
    return jnp.concatenate([pre_ref[...], down_ref[...]], axis=1)


def split_kernel(pre_ref, down_ref, front_out, back_out):
    half = front_out.shape[0]
    edge = pre_ref.shape[1]
    for out, rows in ((front_out, slice(0, half)), (back_out, slice(half, 2 * half))):
        out[:, :edge] = pre_ref[rows, :]
        out[:, edge:] = down_ref[rows, :]


def join_kernel(first, arrived_ref, pre_ref, down_ref, out_ref):
    half = arrived_ref.shape[0]
    chunk = chunk_of(pre_ref, down_ref)
    added, rest = (slice(0, half), slice(half, None)) if first else (slice(half, None), slice(0, half))
    out_ref[added] = f32_sum(arrived_ref[...], chunk[added])
    out_ref[rest] = chunk[rest]


def add_kernel(arrived_ref, pre_ref, down_ref, out_ref):
    out_ref[...] = f32_sum(arrived_ref[...], chunk_of(pre_ref, down_ref))


def finish_kernel(forward_ref, backward_ref, pre_ref, down_ref, gate_out, up_out, down_out):
    forward, backward = forward_ref[...], backward_ref[...]
    if forward.shape != gate_out.shape[1:2] + forward.shape[1:]:
        arrived = jnp.concatenate([forward, backward], axis=0).astype(F32)
    else:
        arrived = forward.astype(F32) + backward.astype(F32)
    total = chunk_of(pre_ref, down_ref).astype(F32) + arrived
    hidden = gate_out.shape[2]
    gate_out[0] = total[:, :hidden].astype(BF16)
    up_out[0] = total[:, hidden : 2 * hidden].astype(BF16)
    down_out[0] = total[:, 2 * hidden :].T.astype(BF16)


class Sums:
    def __init__(self, far, block, chips):
        self.block, self.chips = block, chips
        self.widths = [chunk.shape[1] for chunk in far]
        self.distance = chips // 2
        half = jax.ShapeDtypeStruct((block // 2, sum(self.widths)), BF16)
        self.operands = call(split_kernel, (half, half), [VMEM, VMEM], far, 8, 1, 1)
        self.send(self.operands)

    def specs(self, away):
        place = away % self.chips
        return [pl.BlockSpec((self.block, width), lambda step: (place, 0)) for width in self.widths]

    def send(self, operands):
        self.moving = (next_chip(operands[0], 1), next_chip(operands[1], -1))

    def step(self):
        joins = self.distance == self.chips // 2
        self.distance -= 1
        out = jax.ShapeDtypeStruct((self.block, sum(self.widths)), BF16)
        return [
            call(
                functools.partial(join_kernel, sign > 0) if joins else add_kernel,
                out,
                [VMEM, *self.specs(sign * self.distance)],
                (arrived, *self.parts),
                12, 1, 1, (1,),
            )
            for sign, arrived in zip((1, -1), self.moving)
        ]

    def finish(self, out_shapes, after):
        arrived, _ = lax.optimization_barrier((self.moving, after))
        return call(
            finish_kernel,
            out_shapes,
            [VMEM, VMEM, *self.specs(0)],
            (*arrived, *self.parts),
            12, 1, 1, (1,),
        )


def select_matrix(most, tok_dev, base_ref, picks_ref):
    local = picks_ref[...] - base_ref[0]
    experts, slots = local.shape
    below = jnp.sum((local < 0).astype(F32), axis=1, keepdims=True).astype(I32)
    counter = lax.broadcasted_iota(I32, (most, 1), 0)
    spread = jnp.concatenate(
        [jnp.broadcast_to(local[e : e + 1], (most, slots)) for e in range(experts)], axis=0
    )
    wanted = jnp.concatenate([below[e : e + 1] + counter for e in range(experts)], axis=0)
    position = lax.broadcasted_iota(I32, spread.shape, 1)
    hit = (position == wanted) & (spread >= 0) & (spread < tok_dev)
    token = jnp.sum(jnp.where(hit, spread + 1, 0).astype(F32), axis=1, keepdims=True) - 1.0
    token_range = lax.broadcasted_iota(I32, (spread.shape[0], tok_dev), 1).astype(F32)
    return (token_range == token).astype(F32)


def select_kernel(most, base_ref, picks_ref, tokens_ref, select_ref, out_ref):
    select = select_matrix(most, tokens_ref.shape[0], base_ref, picks_ref).astype(BF16)
    select_ref[...] = select
    out_ref[...] = dot_nn(select, tokens_ref[...]).astype(BF16)


def collect_matrix_kernel(most, base_ref, picks_ref, out_ref):
    out_ref[...] = select_matrix(most, out_ref.shape[0], base_ref, picks_ref).T.astype(BF16)


def gather_kernel(select_ref, tokens_ref, out_ref):
    out_ref[...] = dot_nn(select_ref[...], tokens_ref[...]).astype(BF16)


def take_kernel(most, tok_dev, own_ref, take_ref, turned_ref):
    slots, columns = take_ref.shape
    lane = lax.broadcasted_iota(I32, (1, columns), 1)
    source = jnp.zeros((1, columns), I32)
    for edge in range(most, columns, most):
        source = source + (lane >= edge).astype(I32)
    within = lane - source * most
    own = own_ref[...]
    start = jnp.sum((own < source * tok_dev).astype(F32), axis=0, keepdims=True)
    stop = jnp.sum((own < (source + 1) * tok_dev).astype(F32), axis=0, keepdims=True)
    slot = start + within.astype(F32)
    slot = jnp.where(slot < stop, slot, -1.0)
    slot_range = lax.broadcasted_iota(I32, (slots, columns), 0).astype(F32)
    hot = (slot_range == slot).astype(F32)
    take_ref[...] = hot.astype(BF16)
    turned_ref[...] = hot.T.astype(BF16)


def compact_kernel(chips, place_ref, take_ref, arrived_ref, scale_ref, full_ref, keep_ref, give_ref):
    chip, core = place_ref[0], place_ref[1]
    block = arrived_ref.shape[1] // (2 * chips)
    for k in range(chips):
        columns = slice(2 * k * block, 2 * (k + 1) * block)
        value = dot_nn(take_ref[...], arrived_ref[:, columns])
        full_ref[:, columns] = value.astype(BF16)
        if scale_ref is not None:
            value = value * scale_ref[...]
        even, odd = value[:, :block], value[:, block:]
        where = pl.ds(pl.multiple_of(lax.rem(k - chip + chips, chips) * block, block), block)

        keep_ref[:, where] = jnp.where(core == 0, even, odd).astype(BF16)
        give_ref[:, where] = jnp.where(core == 0, odd, even).astype(BF16)


def plain_compact_kernel(chips, place_ref, take_ref, arrived_ref, full_ref, keep_ref, give_ref):
    compact_kernel(chips, place_ref, take_ref, arrived_ref, None, full_ref, keep_ref, give_ref)


def grad_kernel(
    tile, grads_ref, down_ref, gate_ref, hidden_ref, slope_ref, activated_ref, pre_ref, slot_ref
):
    hidden_width = down_ref.shape[0]
    total = jnp.zeros(slot_ref.shape, F32)
    for begin in range(0, hidden_width, tile):
        columns = slice(begin, begin + tile)
        raw = dot_nt(grads_ref[...], down_ref[columns, :])
        total = total + jnp.sum(raw * hidden_ref[:, columns].astype(F32), axis=1, keepdims=True)
        scaled = raw * gate_ref[...]
        pre_ref[:, columns] = (scaled * slope_ref[:, columns]).astype(BF16)
        other = slice(hidden_width + begin, hidden_width + begin + tile)
        pre_ref[:, other] = (scaled * activated_ref[:, columns]).astype(BF16)
    slot_ref[...] = total


def return_kernel(tile, pre_ref, gate_ref, up_ref, turned_ref, out_ref):
    width, hidden_width = gate_ref.shape
    for begin in range(0, width, tile):
        columns = slice(begin, begin + tile)
        row_grads = dot_nt(pre_ref[:, :hidden_width], gate_ref[columns, :]) + dot_nt(
            pre_ref[:, hidden_width:], up_ref[columns, :]
        )
        out_ref[:, columns] = dot_nn(turned_ref[...], row_grads.astype(BF16)).astype(BF16)


def call(kernel, out_shapes, in_specs, operands, limit_mib, flops, bytes_accessed, grid=()):
    return pl.pallas_call(
        kernel,
        grid=grid,
        out_shape=out_shapes,
        in_specs=in_specs,
        out_specs=jax.tree.map(lambda _: VMEM, out_shapes),
        compiler_params=pltpu.CompilerParams(vmem_limit_bytes=limit_mib * 2**20),
        cost_estimate=pl.CostEstimate(
            flops=flops, bytes_accessed=bytes_accessed, transcendentals=0
        ),
    )(*operands)


def body(tokens, cotangent, picks, gates, w_gate, w_up, w_down):
    node_count = lax.axis_size("expert")
    self_index = lax.axis_index("expert")
    dp_size = lax.axis_size("dp")
    dp_index = lax.axis_index("dp")
    chips = dp_size // 2
    place = jnp.stack([lax.shift_right_logical(dp_index, 1), dp_index & 1]).astype(I32)
    tok_dev, width = tokens.shape
    slot_count = gates.shape[2]
    most = max(2, 3 * slot_count // (2 * node_count))
    padded = node_count * most
    hidden_width = w_gate.shape[2]
    block = width // dp_size

    def shape(*dims, dtype=BF16):
        return jax.ShapeDtypeStruct(dims, dtype)

    table = picks[0]
    base = (self_index * tok_dev).astype(I32).reshape(1)
    select, out_rows = call(
        lambda *refs: select_kernel(most, *refs),
        (shape(padded, tok_dev), shape(padded, width)),
        [SMEM, VMEM, VMEM],
        (base, table, tokens),
        16, 2 * padded * tok_dev * width, 4 * padded * width,
    )
    out_grads = call(
        gather_kernel,
        shape(padded, width),
        [VMEM, VMEM],
        (select, cotangent),
        16, 2 * padded * tok_dev * width, 4 * padded * width,
    )

    def exchange(array):
        shaped = array.reshape(node_count, most, width)
        return lax.all_to_all(shaped, "expert", 0, 0, tiled=True).reshape(padded, width)

    arrived_rows = exchange(out_rows)
    arrived_grads = exchange(out_grads)

    own = lax.dynamic_index_in_dim(table, self_index, 0, keepdims=False)
    take, take_turned = call(
        lambda *refs: take_kernel(most, tok_dev, *refs),
        (shape(slot_count, padded), shape(padded, slot_count)),
        [VMEM],
        (own.reshape(slot_count, 1),),
        8, 8 * slot_count * padded, 2 * slot_count * padded,
    )
    select_turned = call(
        functools.partial(collect_matrix_kernel, most),
        shape(tok_dev, padded),
        [SMEM, VMEM],
        (base, table),
        8, 8 * slot_count * padded, 2 * slot_count * padded,
    )
    compact_shapes = (
        shape(slot_count, width), shape(slot_count, width // 2), shape(slot_count, width // 2)
    )
    compact_cost = (12, 2 * slot_count * padded * width, 8 * slot_count * width)
    rows, rows_keep, rows_give = call(
        lambda *refs: plain_compact_kernel(chips, *refs),
        compact_shapes,
        [SMEM, VMEM, VMEM],
        (place, take, arrived_rows),
        *compact_cost,
    )
    rows_both = jnp.concatenate([rows_keep, swap_cores(rows_give)], axis=0)
    gate_pre = dot_nn(rows, w_gate[0])
    up_pre = dot_nn(rows, w_up[0])
    sigmoid_gate = jax.nn.sigmoid(gate_pre)
    activated = gate_pre * sigmoid_gate
    slope = up_pre * sigmoid_gate * (1.0 + gate_pre * (1.0 - sigmoid_gate))
    hidden = (activated * up_pre).astype(BF16)
    hidden_both = jnp.concatenate([hidden, swap_cores(hidden)], axis=0)

    gate_rows = gates.reshape(slot_count, 1)
    arrived_grads, hidden, slope, activated, rows_both, hidden_both = lax.optimization_barrier(
        (arrived_grads, hidden, slope, activated, rows_both, hidden_both)
    )
    grads, scaled_keep, scaled_give = call(
        lambda *refs: compact_kernel(chips, *refs),
        compact_shapes,
        [SMEM, VMEM, VMEM, VMEM],
        (place, take, arrived_grads, gate_rows),
        *compact_cost,
    )
    scaled_both = jnp.concatenate([scaled_keep, swap_cores(scaled_give)], axis=0)
    pre_grads, slot_grads = call(
        lambda *refs: grad_kernel(min(256, hidden_width), *refs),
        (shape(slot_count, 2 * hidden_width), shape(slot_count, 1, dtype=F32)),
        [VMEM] * 6,
        (grads, w_down[0], gate_rows, hidden, slope, activated),
        16, 2 * slot_count * width * hidden_width, 2 * width * hidden_width,
    )
    pre_both = jnp.concatenate([pre_grads, swap_cores(pre_grads)], axis=0)

    def parts_of(columns, after=None):
        sources = (rows_both, pre_both, scaled_both, hidden_both)
        if after is not None:
            sources, _ = lax.optimization_barrier((sources, after))
        return (
            dot_tn(sources[0][:, columns], sources[1]).astype(BF16),
            dot_tn(sources[2][:, columns], sources[3]).astype(BF16),
        )

    def give_back(pre_grads):
        return call(
            lambda *refs: return_kernel(min(256, width), *refs),
            shape(padded, width),
            [VMEM] * 4,
            (pre_grads, w_gate[0], w_up[0], take_turned),
            16, 4 * slot_count * width * hidden_width, 4 * width * hidden_width,
        )

    def collect(came_back):
        return call(
            gather_kernel,
            shape(tok_dev, width),
            [VMEM, VMEM],
            (select_turned, came_back),
            12, 2 * padded * tok_dev * width, 4 * padded * width,
        )

    if chips > 1:
        farthest = chips // 2
        far = parts_of(slice(farthest * block, (farthest + 1) * block))
        sums = Sums(far, block, chips)
        sums.parts = parts_of(slice(None), sums.operands)
        returning = give_back(pre_grads)
        returned = None
        while sums.distance > 1:
            operands = sums.step()
            if returned is None:
                returning, _ = lax.optimization_barrier((returning, operands))
                returned = exchange(returning)
            sums.send(operands)
            latest = operands
        if returned is None:
            returned, latest = exchange(returning), returning
        returned, _ = lax.optimization_barrier((returned, latest))
        token_grads = collect(returned)
        weight_shapes = (
            shape(1, block, hidden_width),
            shape(1, block, hidden_width),
            shape(1, hidden_width, block),
        )
        weight_grads = sums.finish(weight_shapes, token_grads)
    else:
        token_grads = collect(exchange(give_back(pre_grads)))
        pre_part, down_part = parts_of(slice(None))
        weight_grads = (*(half[None] for half in jnp.split(pre_part, 2, axis=1)), down_part.T[None])
    return (token_grads, slot_grads.reshape(1, 1, slot_count), *weight_grads)


def solution(mesh):
    return jax.shard_map(
        body,
        mesh=mesh,
        in_specs=(
            P(("dp", "expert"), None),
            P(("dp", "expert"), None),
            P("dp", None, None),
            P("dp", "expert", None),
            P("expert", None, None),
            P("expert", None, None),
            P("expert", None, None),
        ),
        out_specs=(
            P(("dp", "expert"), None),
            P("dp", "expert", None),
            P("expert", "dp", None),
            P("expert", "dp", None),
            P("expert", None, "dp"),
        ),
        check_vma=False,
    )
```

```python
import functools

import jax
import jax.numpy as jnp
from jax import lax
from jax.experimental import pallas as pl
from jax.experimental.pallas import tpu as pltpu
from jax.sharding import PartitionSpec as P

BF16 = jnp.bfloat16
F32 = jnp.float32
I32 = jnp.int32
VMEM = pl.BlockSpec(memory_space=pltpu.VMEM)
SMEM = pl.BlockSpec(memory_space=pltpu.SMEM)


def dot_nn(left, right):
    return jnp.dot(left, right, preferred_element_type=F32)


def dot_nt(left, right):
    return lax.dot_general(left, right, (((1,), (1,)), ((), ())), preferred_element_type=F32)


def dot_tn(left, right):
    return lax.dot_general(left, right, (((0,), (0,)), ((), ())), preferred_element_type=F32)


def swap_cores(array):
    size = lax.axis_size("dp")
    return lax.ppermute(array, "dp", [(i, i ^ 1) for i in range(size)])


def next_chip(array, sign):
    size = lax.axis_size("dp")
    return lax.ppermute(array, "dp", [(i, (i + 2 * sign) % size) for i in range(size)])


def f32_sum(*terms):
    total = terms[0].astype(F32)
    for term in terms[1:]:
        total = total + term.astype(F32)
    return total.astype(BF16)


def chunk_of(pre_ref, down_ref):
    return jnp.concatenate([pre_ref[...], down_ref[...]], axis=1)


def split_kernel(pre_ref, down_ref, front_out, back_out):
    half = front_out.shape[0]
    edge = pre_ref.shape[1]
    for out, rows in ((front_out, slice(0, half)), (back_out, slice(half, 2 * half))):
        out[:, :edge] = pre_ref[rows, :]
        out[:, edge:] = down_ref[rows, :]


def join_kernel(first, arrived_ref, pre_ref, down_ref, out_ref):
    half = arrived_ref.shape[0]
    chunk = chunk_of(pre_ref, down_ref)
    added, rest = (slice(0, half), slice(half, None)) if first else (slice(half, None), slice(0, half))
    out_ref[added] = f32_sum(arrived_ref[...], chunk[added])
    out_ref[rest] = chunk[rest]


def add_kernel(arrived_ref, pre_ref, down_ref, out_ref):
    out_ref[...] = f32_sum(arrived_ref[...], chunk_of(pre_ref, down_ref))


def finish_kernel(forward_ref, backward_ref, pre_ref, down_ref, gate_out, up_out, down_out):
    forward, backward = forward_ref[...], backward_ref[...]
    if forward.shape != gate_out.shape[1:2] + forward.shape[1:]:
        arrived = jnp.concatenate([forward, backward], axis=0).astype(F32)
    else:
        arrived = forward.astype(F32) + backward.astype(F32)
    total = chunk_of(pre_ref, down_ref).astype(F32) + arrived
    hidden = gate_out.shape[2]
    gate_out[0] = total[:, :hidden].astype(BF16)
    up_out[0] = total[:, hidden : 2 * hidden].astype(BF16)
    down_out[0] = total[:, 2 * hidden :].astype(BF16).T


class Sums:
    def __init__(self, far, block, chips):
        self.block, self.chips = block, chips
        self.widths = [chunk.shape[1] for chunk in far]
        self.distance = chips // 2
        half = jax.ShapeDtypeStruct((block // 2, sum(self.widths)), BF16)
        self.operands = call(split_kernel, (half, half), [VMEM, VMEM], far, 8, 1, 1)
        self.send(self.operands)

    def specs(self, away):
        place = away % self.chips
        return [pl.BlockSpec((self.block, width), lambda step: (place, 0)) for width in self.widths]

    def send(self, operands):
        self.moving = (next_chip(operands[0], 1), next_chip(operands[1], -1))

    def step(self):
        joins = self.distance == self.chips // 2
        self.distance -= 1
        out = jax.ShapeDtypeStruct((self.block, sum(self.widths)), BF16)
        return [
            call(
                functools.partial(join_kernel, sign > 0) if joins else add_kernel,
                out,
                [VMEM, *self.specs(sign * self.distance)],
                (arrived, *self.parts),
                54 if self.distance == self.chips // 2 - 2 else 12, 1, 1, (1,),
            )
            for sign, arrived in zip((1, -1), self.moving)
        ]

    def finish(self, out_shapes, after):
        arrived, _ = lax.optimization_barrier((self.moving, after))
        return call(
            finish_kernel,
            out_shapes,
            [VMEM, VMEM, *self.specs(0)],
            (*arrived, *self.parts),
            12, 1, 1, (1,),
        )


def select_matrix(most, tok_dev, base_ref, picks_ref):
    local = picks_ref[...] - base_ref[0]
    experts, slots = local.shape
    below = jnp.sum((local < 0).astype(F32), axis=1, keepdims=True).astype(I32)
    counter = lax.broadcasted_iota(I32, (most, 1), 0)
    spread = jnp.concatenate(
        [jnp.broadcast_to(local[e : e + 1], (most, slots)) for e in range(experts)], axis=0
    )
    wanted = jnp.concatenate([below[e : e + 1] + counter for e in range(experts)], axis=0)
    position = lax.broadcasted_iota(I32, spread.shape, 1)
    hit = (position == wanted) & (spread >= 0) & (spread < tok_dev)
    token = jnp.sum(jnp.where(hit, spread + 1, 0).astype(F32), axis=1, keepdims=True) - 1.0
    token_range = lax.broadcasted_iota(I32, (spread.shape[0], tok_dev), 1).astype(F32)
    return (token_range == token).astype(F32)


def select_kernel(most, base_ref, picks_ref, tokens_ref, select_ref, out_ref):
    select = select_matrix(most, tokens_ref.shape[0], base_ref, picks_ref).astype(BF16)
    select_ref[...] = select
    out_ref[...] = dot_nn(select, tokens_ref[...]).astype(BF16)


def collect_matrix_kernel(most, base_ref, picks_ref, out_ref):
    out_ref[...] = select_matrix(most, out_ref.shape[0], base_ref, picks_ref).T.astype(BF16)


def gather_kernel(select_ref, tokens_ref, out_ref):
    out_ref[...] = dot_nn(select_ref[...], tokens_ref[...]).astype(BF16)


def take_kernel(most, tok_dev, own_ref, take_ref, turned_ref):
    slots, columns = take_ref.shape
    lane = lax.broadcasted_iota(I32, (1, columns), 1)
    source = jnp.zeros((1, columns), I32)
    for edge in range(most, columns, most):
        source = source + (lane >= edge).astype(I32)
    within = lane - source * most
    own = own_ref[...]
    start = jnp.sum((own < source * tok_dev).astype(F32), axis=0, keepdims=True)
    stop = jnp.sum((own < (source + 1) * tok_dev).astype(F32), axis=0, keepdims=True)
    slot = start + within.astype(F32)
    slot = jnp.where(slot < stop, slot, -1.0)
    slot_range = lax.broadcasted_iota(I32, (slots, columns), 0).astype(F32)
    hot = (slot_range == slot).astype(F32)
    take_ref[...] = hot.astype(BF16)
    turned_ref[...] = hot.T.astype(BF16)


def compact_kernel(chips, place_ref, take_ref, arrived_ref, scale_ref, full_ref, keep_ref, give_ref):
    chip, core = place_ref[0], place_ref[1]
    block = arrived_ref.shape[1] // (2 * chips)
    for k in range(chips):
        columns = slice(2 * k * block, 2 * (k + 1) * block)
        value = dot_nn(take_ref[...], arrived_ref[:, columns])
        full_ref[:, columns] = value.astype(BF16)
        if scale_ref is not None:
            value = value * scale_ref[...]
        even, odd = value[:, :block], value[:, block:]
        where = pl.ds(pl.multiple_of(lax.rem(k - chip + chips, chips) * block, block), block)

        keep_ref[:, where] = jnp.where(core == 0, even, odd).astype(BF16)
        give_ref[:, where] = jnp.where(core == 0, odd, even).astype(BF16)


def plain_compact_kernel(chips, place_ref, take_ref, arrived_ref, full_ref, keep_ref, give_ref):
    compact_kernel(chips, place_ref, take_ref, arrived_ref, None, full_ref, keep_ref, give_ref)


def grad_kernel(
    tile, grads_ref, down_ref, gate_ref, hidden_ref, slope_ref, activated_ref, pre_ref, slot_ref
):
    hidden_width = down_ref.shape[0]
    total = jnp.zeros(slot_ref.shape, F32)
    for begin in range(0, hidden_width, tile):
        columns = slice(begin, begin + tile)
        raw = dot_nt(grads_ref[...], down_ref[columns, :])
        total = total + jnp.sum(raw * hidden_ref[:, columns].astype(F32), axis=1, keepdims=True)
        scaled = raw * gate_ref[...]
        pre_ref[:, columns] = (scaled * slope_ref[:, columns]).astype(BF16)
        other = slice(hidden_width + begin, hidden_width + begin + tile)
        pre_ref[:, other] = (scaled * activated_ref[:, columns]).astype(BF16)
    slot_ref[...] = total


def return_kernel(tile, pre_ref, gate_ref, up_ref, turned_ref, out_ref):
    width, hidden_width = gate_ref.shape
    for begin in range(0, width, tile):
        columns = slice(begin, begin + tile)
        row_grads = dot_nt(pre_ref[:, :hidden_width], gate_ref[columns, :]) + dot_nt(
            pre_ref[:, hidden_width:], up_ref[columns, :]
        )
        out_ref[:, columns] = dot_nn(turned_ref[...], row_grads.astype(BF16)).astype(BF16)


def call(kernel, out_shapes, in_specs, operands, limit_mib, flops, bytes_accessed, grid=()):
    return pl.pallas_call(
        kernel,
        grid=grid,
        out_shape=out_shapes,
        in_specs=in_specs,
        out_specs=jax.tree.map(lambda _: VMEM, out_shapes),
        compiler_params=pltpu.CompilerParams(vmem_limit_bytes=limit_mib * 2**20),
        cost_estimate=pl.CostEstimate(
            flops=flops, bytes_accessed=bytes_accessed, transcendentals=0
        ),
    )(*operands)


def body(tokens, cotangent, picks, gates, w_gate, w_up, w_down):
    node_count = lax.axis_size("expert")
    self_index = lax.axis_index("expert")
    dp_size = lax.axis_size("dp")
    dp_index = lax.axis_index("dp")
    chips = dp_size // 2
    place = jnp.stack([lax.shift_right_logical(dp_index, 1), dp_index & 1]).astype(I32)
    tok_dev, width = tokens.shape
    slot_count = gates.shape[2]
    most = max(2, 3 * slot_count // (2 * node_count))
    padded = node_count * most
    hidden_width = w_gate.shape[2]
    block = width // dp_size

    def shape(*dims, dtype=BF16):
        return jax.ShapeDtypeStruct(dims, dtype)

    table = picks[0]
    base = (self_index * tok_dev).astype(I32).reshape(1)
    select, out_rows = call(
        lambda *refs: select_kernel(most, *refs),
        (shape(padded, tok_dev), shape(padded, width)),
        [SMEM, VMEM, VMEM],
        (base, table, tokens),
        16, 2 * padded * tok_dev * width, 4 * padded * width,
    )
    out_grads = call(
        gather_kernel,
        shape(padded, width),
        [VMEM, VMEM],
        (select, cotangent),
        16, 2 * padded * tok_dev * width, 4 * padded * width,
    )

    def exchange(array):
        shaped = array.reshape(node_count, most, width)
        return lax.all_to_all(shaped, "expert", 0, 0, tiled=True).reshape(padded, width)

    arrived_rows = exchange(out_rows)
    arrived_grads = exchange(out_grads)

    own = lax.dynamic_index_in_dim(table, self_index, 0, keepdims=False)
    take, take_turned = call(
        lambda *refs: take_kernel(most, tok_dev, *refs),
        (shape(slot_count, padded), shape(padded, slot_count)),
        [VMEM],
        (own.reshape(slot_count, 1),),
        8, 8 * slot_count * padded, 2 * slot_count * padded,
    )
    select_turned = call(
        functools.partial(collect_matrix_kernel, most),
        shape(tok_dev, padded),
        [SMEM, VMEM],
        (base, table),
        8, 8 * slot_count * padded, 2 * slot_count * padded,
    )
    compact_shapes = (
        shape(slot_count, width), shape(slot_count, width // 2), shape(slot_count, width // 2)
    )
    compact_cost = (12, 2 * slot_count * padded * width, 8 * slot_count * width)
    rows, rows_keep, rows_give = call(
        lambda *refs: plain_compact_kernel(chips, *refs),
        compact_shapes,
        [SMEM, VMEM, VMEM],
        (place, take, arrived_rows),
        *compact_cost,
    )
    rows_got = swap_cores(rows_give)
    gate_pre = dot_nn(rows, w_gate[0])
    up_pre = dot_nn(rows, w_up[0])
    sigmoid_gate = jax.nn.sigmoid(gate_pre)
    activated = gate_pre * sigmoid_gate
    slope = up_pre * sigmoid_gate * (1.0 + gate_pre * (1.0 - sigmoid_gate))
    hidden = (activated * up_pre).astype(BF16)
    hidden_got = swap_cores(hidden)

    gate_rows = gates.reshape(slot_count, 1)
    arrived_grads, hidden, slope, activated, rows_got, hidden_got = lax.optimization_barrier(
        (arrived_grads, hidden, slope, activated, rows_got, hidden_got)
    )
    grads, scaled_keep, scaled_give = call(
        lambda *refs: compact_kernel(chips, *refs),
        compact_shapes,
        [SMEM, VMEM, VMEM, VMEM],
        (place, take, arrived_grads, gate_rows),
        *compact_cost,
    )
    scaled_both = jnp.concatenate([scaled_keep, swap_cores(scaled_give)], axis=0)
    pre_grads, slot_grads = call(
        lambda *refs: grad_kernel(min(256, hidden_width), *refs),
        (shape(slot_count, 2 * hidden_width), shape(slot_count, 1, dtype=F32)),
        [VMEM] * 6,
        (grads, w_down[0], gate_rows, hidden, slope, activated),
        16, 2 * slot_count * width * hidden_width, 2 * width * hidden_width,
    )
    late_sides, _ = lax.optimization_barrier(((rows_keep, rows_got, hidden, hidden_got), pre_grads))
    rows_both = jnp.concatenate(late_sides[:2], axis=0)
    hidden_both = jnp.concatenate(late_sides[2:], axis=0)
    pre_both = jnp.concatenate([pre_grads, swap_cores(pre_grads)], axis=0)

    def parts_of(columns, after=None):
        sources = (rows_both, pre_both, scaled_both, hidden_both)
        if after is not None:
            sources, _ = lax.optimization_barrier((sources, after))
        return (
            dot_tn(sources[0][:, columns], sources[1]).astype(BF16),
            dot_tn(sources[2][:, columns], sources[3]).astype(BF16),
        )

    def give_back(pre_grads):
        return call(
            lambda *refs: return_kernel(min(256, width), *refs),
            shape(padded, width),
            [VMEM] * 4,
            (pre_grads, w_gate[0], w_up[0], take_turned),
            16, 4 * slot_count * width * hidden_width, 4 * width * hidden_width,
        )

    def collect(came_back):
        return call(
            gather_kernel,
            shape(tok_dev, width),
            [VMEM, VMEM],
            (select_turned, came_back),
            12, 2 * padded * tok_dev * width, 4 * padded * width,
        )

    if chips > 1:
        farthest = chips // 2
        far = parts_of(slice(farthest * block, (farthest + 1) * block))
        sums = Sums(far, block, chips)
        sums.parts = parts_of(slice(None), sums.operands)
        returning = give_back(pre_grads)
        returned = None
        while sums.distance > 1:
            operands = sums.step()
            if returned is None:
                returning, _ = lax.optimization_barrier((returning, operands))
                returned = exchange(returning)
            sums.send(operands)
            latest = operands
        if returned is None:
            returned, latest = exchange(returning), returning
        returned, _ = lax.optimization_barrier((returned, latest))
        token_grads = collect(returned)
        weight_shapes = (
            shape(1, block, hidden_width),
            shape(1, block, hidden_width),
            shape(1, hidden_width, block),
        )
        weight_grads = sums.finish(weight_shapes, token_grads)
    else:
        token_grads = collect(exchange(give_back(pre_grads)))
        pre_part, down_part = parts_of(slice(None))
        weight_grads = (*(half[None] for half in jnp.split(pre_part, 2, axis=1)), down_part.T[None])
    return (token_grads, slot_grads.reshape(1, 1, slot_count), *weight_grads)


def solution(mesh):
    return jax.shard_map(
        body,
        mesh=mesh,
        in_specs=(
            P(("dp", "expert"), None),
            P(("dp", "expert"), None),
            P("dp", None, None),
            P("dp", "expert", None),
            P("expert", None, None),
            P("expert", None, None),
            P("expert", None, None),
        ),
        out_specs=(
            P(("dp", "expert"), None),
            P("dp", "expert", None),
            P("expert", "dp", None),
            P("expert", "dp", None),
            P("expert", None, "dp"),
        ),
        check_vma=False,
    )
```

```python
import functools

import jax
import jax.numpy as jnp
from jax import lax
from jax.experimental import pallas as pl
from jax.experimental.pallas import tpu as pltpu
from jax.sharding import PartitionSpec as P

BF16 = jnp.bfloat16
F32 = jnp.float32
I32 = jnp.int32
VMEM = pl.BlockSpec(memory_space=pltpu.VMEM)
SMEM = pl.BlockSpec(memory_space=pltpu.SMEM)


def dot_nn(left, right):
    return jnp.dot(left, right, preferred_element_type=F32)


def dot_nt(left, right):
    return lax.dot_general(left, right, (((1,), (1,)), ((), ())), preferred_element_type=F32)


def dot_tn(left, right):
    return lax.dot_general(left, right, (((0,), (0,)), ((), ())), preferred_element_type=F32)


def swap_cores(array):
    size = lax.axis_size("dp")
    return lax.ppermute(array, "dp", [(i, i ^ 1) for i in range(size)])


def next_chip(array, sign):
    size = lax.axis_size("dp")
    return lax.ppermute(array, "dp", [(i, (i + 2 * sign) % size) for i in range(size)])


def f32_sum(*terms):
    total = terms[0].astype(F32)
    for term in terms[1:]:
        total = total + term.astype(F32)
    return total.astype(BF16)


def chunk_of(pre_ref, down_ref):
    return jnp.concatenate([pre_ref[...], down_ref[...]], axis=1)


def split_kernel(pre_ref, down_ref, front_out, back_out):
    half = front_out.shape[0]
    edge = pre_ref.shape[1]
    for out, rows in ((front_out, slice(0, half)), (back_out, slice(half, 2 * half))):
        out[:, :edge] = pre_ref[rows, :]
        out[:, edge:] = down_ref[rows, :]


def join_kernel(first, arrived_ref, pre_ref, down_ref, out_ref):
    half = arrived_ref.shape[0]
    chunk = chunk_of(pre_ref, down_ref)
    added, rest = (slice(0, half), slice(half, None)) if first else (slice(half, None), slice(0, half))
    out_ref[added] = f32_sum(arrived_ref[...], chunk[added])
    out_ref[rest] = chunk[rest]


def add_kernel(arrived_ref, pre_ref, down_ref, out_ref):
    out_ref[...] = f32_sum(arrived_ref[...], chunk_of(pre_ref, down_ref))


def finish_kernel(forward_ref, backward_ref, pre_ref, down_ref, gate_out, up_out, down_out):
    forward, backward = forward_ref[...], backward_ref[...]
    if forward.shape != gate_out.shape[1:2] + forward.shape[1:]:
        arrived = jnp.concatenate([forward, backward], axis=0).astype(F32)
    else:
        arrived = forward.astype(F32) + backward.astype(F32)
    total = chunk_of(pre_ref, down_ref).astype(F32) + arrived
    hidden = gate_out.shape[2]
    gate_out[0] = total[:, :hidden].astype(BF16)
    up_out[0] = total[:, hidden : 2 * hidden].astype(BF16)
    down_out[0] = total[:, 2 * hidden :].T.astype(BF16)


class Sums:
    def __init__(self, far, block, chips):
        self.block, self.chips = block, chips
        self.widths = [chunk.shape[1] for chunk in far]
        self.distance = chips // 2
        half = jax.ShapeDtypeStruct((block // 2, sum(self.widths)), BF16)
        self.operands = call(split_kernel, (half, half), [VMEM, VMEM], far, 8, 1, 1)
        self.send(self.operands)

    def specs(self, away):
        place = away % self.chips
        return [pl.BlockSpec((self.block, width), lambda step: (place, 0)) for width in self.widths]

    def send(self, operands):
        self.moving = (next_chip(operands[0], 1), next_chip(operands[1], -1))

    def step(self):
        joins = self.distance == self.chips // 2
        self.distance -= 1
        out = jax.ShapeDtypeStruct((self.block, sum(self.widths)), BF16)
        return [
            call(
                functools.partial(join_kernel, sign > 0) if joins else add_kernel,
                out,
                [VMEM, *self.specs(sign * self.distance)],
                (arrived, *self.parts),
                12, 1, 1, (1,),
            )
            for sign, arrived in zip((1, -1), self.moving)
        ]

    def finish(self, out_shapes, after):
        arrived, _ = lax.optimization_barrier((self.moving, after))
        return call(
            finish_kernel,
            out_shapes,
            [VMEM, VMEM, *self.specs(0)],
            (*arrived, *self.parts),
            12, 1, 1, (1,),
        )


def select_matrix(most, tok_dev, base_ref, picks_ref):
    local = picks_ref[...] - base_ref[0]
    experts, slots = local.shape
    below = jnp.sum((local < 0).astype(F32), axis=1, keepdims=True).astype(I32)
    counter = lax.broadcasted_iota(I32, (most, 1), 0)
    spread = jnp.concatenate(
        [jnp.broadcast_to(local[e : e + 1], (most, slots)) for e in range(experts)], axis=0
    )
    wanted = jnp.concatenate([below[e : e + 1] + counter for e in range(experts)], axis=0)
    position = lax.broadcasted_iota(I32, spread.shape, 1)
    hit = (position == wanted) & (spread >= 0) & (spread < tok_dev)
    token = jnp.sum(jnp.where(hit, spread + 1, 0).astype(F32), axis=1, keepdims=True) - 1.0
    token_range = lax.broadcasted_iota(I32, (spread.shape[0], tok_dev), 1).astype(F32)
    return (token_range == token).astype(F32)


def select_kernel(most, base_ref, picks_ref, tokens_ref, select_ref, out_ref):
    select = select_matrix(most, tokens_ref.shape[0], base_ref, picks_ref).astype(BF16)
    select_ref[...] = select
    out_ref[...] = dot_nn(select, tokens_ref[...]).astype(BF16)


def collect_matrix_kernel(most, base_ref, picks_ref, out_ref):
    out_ref[...] = select_matrix(most, out_ref.shape[0], base_ref, picks_ref).T.astype(BF16)


def gather_kernel(select_ref, tokens_ref, out_ref):
    out_ref[...] = dot_nn(select_ref[...], tokens_ref[...]).astype(BF16)


def take_kernel(most, tok_dev, own_ref, take_ref, turned_ref):
    slots, columns = take_ref.shape
    lane = lax.broadcasted_iota(I32, (1, columns), 1)
    source = jnp.zeros((1, columns), I32)
    for edge in range(most, columns, most):
        source = source + (lane >= edge).astype(I32)
    within = lane - source * most
    own = own_ref[...]
    start = jnp.sum((own < source * tok_dev).astype(F32), axis=0, keepdims=True)
    stop = jnp.sum((own < (source + 1) * tok_dev).astype(F32), axis=0, keepdims=True)
    slot = start + within.astype(F32)
    slot = jnp.where(slot < stop, slot, -1.0)
    slot_range = lax.broadcasted_iota(I32, (slots, columns), 0).astype(F32)
    hot = (slot_range == slot).astype(F32)
    take_ref[...] = hot.astype(BF16)
    turned_ref[...] = hot.T.astype(BF16)


def compact_kernel(chips, place_ref, take_ref, arrived_ref, scale_ref, full_ref, keep_ref, give_ref):
    chip, core = place_ref[0], place_ref[1]
    block = arrived_ref.shape[1] // (2 * chips)
    for k in range(chips):
        columns = slice(2 * k * block, 2 * (k + 1) * block)
        value = dot_nn(take_ref[...], arrived_ref[:, columns])
        full_ref[:, columns] = value.astype(BF16)
        if scale_ref is not None:
            value = value * scale_ref[...]
        even, odd = value[:, :block], value[:, block:]
        where = pl.ds(pl.multiple_of(lax.rem(k - chip + chips, chips) * block, block), block)

        keep_ref[:, where] = jnp.where(core == 0, even, odd).astype(BF16)
        give_ref[:, where] = jnp.where(core == 0, odd, even).astype(BF16)


def plain_compact_kernel(chips, place_ref, take_ref, arrived_ref, full_ref, keep_ref, give_ref):
    compact_kernel(chips, place_ref, take_ref, arrived_ref, None, full_ref, keep_ref, give_ref)


def grad_kernel(
    tile, grads_ref, down_ref, gate_ref, hidden_ref, slope_ref, activated_ref, pre_ref, slot_ref
):
    hidden_width = down_ref.shape[0]
    total = jnp.zeros(slot_ref.shape, F32)
    for begin in range(0, hidden_width, tile):
        columns = slice(begin, begin + tile)
        raw = dot_nt(grads_ref[...], down_ref[columns, :])
        total = total + jnp.sum(raw * hidden_ref[:, columns].astype(F32), axis=1, keepdims=True)
        scaled = raw * gate_ref[...]
        pre_ref[:, columns] = (scaled * slope_ref[:, columns]).astype(BF16)
        other = slice(hidden_width + begin, hidden_width + begin + tile)
        pre_ref[:, other] = (scaled * activated_ref[:, columns]).astype(BF16)
    slot_ref[...] = total


def return_kernel(tile, pre_ref, gate_ref, up_ref, turned_ref, out_ref):
    width, hidden_width = gate_ref.shape
    for begin in range(0, width, tile):
        columns = slice(begin, begin + tile)
        row_grads = dot_nt(pre_ref[:, :hidden_width], gate_ref[columns, :]) + dot_nt(
            pre_ref[:, hidden_width:], up_ref[columns, :]
        )
        out_ref[:, columns] = dot_nn(turned_ref[...], row_grads.astype(BF16)).astype(BF16)


def call(kernel, out_shapes, in_specs, operands, limit_mib, flops, bytes_accessed, grid=()):
    return pl.pallas_call(
        kernel,
        grid=grid,
        out_shape=out_shapes,
        in_specs=in_specs,
        out_specs=jax.tree.map(lambda _: VMEM, out_shapes),
        compiler_params=pltpu.CompilerParams(vmem_limit_bytes=limit_mib * 2**20),
        cost_estimate=pl.CostEstimate(
            flops=flops, bytes_accessed=bytes_accessed, transcendentals=0
        ),
    )(*operands)


def body(tokens, cotangent, picks, gates, w_gate, w_up, w_down):
    node_count = lax.axis_size("expert")
    self_index = lax.axis_index("expert")
    dp_size = lax.axis_size("dp")
    dp_index = lax.axis_index("dp")
    chips = dp_size // 2
    place = jnp.stack([lax.shift_right_logical(dp_index, 1), dp_index & 1]).astype(I32)
    tok_dev, width = tokens.shape
    slot_count = gates.shape[2]
    most = max(2, 3 * slot_count // (2 * node_count))
    padded = node_count * most
    hidden_width = w_gate.shape[2]
    block = width // dp_size

    def shape(*dims, dtype=BF16):
        return jax.ShapeDtypeStruct(dims, dtype)

    table = picks[0]
    base = (self_index * tok_dev).astype(I32).reshape(1)
    origin = lambda step: (0, 0)
    select, out_rows = call(
        lambda *refs: select_kernel(most, *refs),
        (shape(padded, tok_dev), shape(padded, width)),
        [SMEM, pl.BlockSpec(table.shape, origin), pl.BlockSpec(tokens.shape, origin)],
        (base, table, tokens),
        54, 2 * padded * tok_dev * width, 4 * padded * width, (1,),
    )
    out_grads = call(
        gather_kernel,
        shape(padded, width),
        [VMEM, VMEM],
        (select, cotangent),
        16, 2 * padded * tok_dev * width, 4 * padded * width,
    )

    def exchange(array):
        shaped = array.reshape(node_count, most, width)
        return lax.all_to_all(shaped, "expert", 0, 0, tiled=True).reshape(padded, width)

    arrived_rows = exchange(out_rows)
    arrived_grads = exchange(out_grads)

    own = lax.dynamic_index_in_dim(table, self_index, 0, keepdims=False)
    take, take_turned = call(
        lambda *refs: take_kernel(most, tok_dev, *refs),
        (shape(slot_count, padded), shape(padded, slot_count)),
        [VMEM],
        (own.reshape(slot_count, 1),),
        8, 8 * slot_count * padded, 2 * slot_count * padded,
    )
    select_turned = call(
        functools.partial(collect_matrix_kernel, most),
        shape(tok_dev, padded),
        [SMEM, VMEM],
        (base, table),
        8, 8 * slot_count * padded, 2 * slot_count * padded,
    )
    compact_shapes = (
        shape(slot_count, width), shape(slot_count, width // 2), shape(slot_count, width // 2)
    )
    compact_cost = (12, 2 * slot_count * padded * width, 8 * slot_count * width)
    rows, rows_keep, rows_give = call(
        lambda *refs: plain_compact_kernel(chips, *refs),
        compact_shapes,
        [SMEM, VMEM, VMEM],
        (place, take, arrived_rows),
        *compact_cost,
    )
    rows_both = jnp.concatenate([rows_keep, swap_cores(rows_give)], axis=0)
    gate_pre = dot_nn(rows, w_gate[0])
    up_pre = dot_nn(rows, w_up[0])
    sigmoid_gate = jax.nn.sigmoid(gate_pre)
    activated = gate_pre * sigmoid_gate
    slope = up_pre * sigmoid_gate * (1.0 + gate_pre * (1.0 - sigmoid_gate))
    hidden = (activated * up_pre).astype(BF16)
    hidden_both = jnp.concatenate([hidden, swap_cores(hidden)], axis=0)

    gate_rows = gates.reshape(slot_count, 1)
    arrived_grads, hidden, slope, activated, rows_both, hidden_both = lax.optimization_barrier(
        (arrived_grads, hidden, slope, activated, rows_both, hidden_both)
    )
    grads, scaled_keep, scaled_give = call(
        lambda *refs: compact_kernel(chips, *refs),
        compact_shapes,
        [SMEM, VMEM, VMEM, VMEM],
        (place, take, arrived_grads, gate_rows),
        *compact_cost,
    )
    scaled_both = jnp.concatenate([scaled_keep, swap_cores(scaled_give)], axis=0)
    pre_grads, slot_grads = call(
        lambda *refs: grad_kernel(min(256, hidden_width), *refs),
        (shape(slot_count, 2 * hidden_width), shape(slot_count, 1, dtype=F32)),
        [VMEM] * 6,
        (grads, w_down[0], gate_rows, hidden, slope, activated),
        16, 2 * slot_count * width * hidden_width, 2 * width * hidden_width,
    )
    pre_both = jnp.concatenate([pre_grads, swap_cores(pre_grads)], axis=0)

    def parts_of(columns, after=None):
        sources = (rows_both, pre_both, scaled_both, hidden_both)
        if after is not None:
            sources, _ = lax.optimization_barrier((sources, after))
        return (
            dot_tn(sources[0][:, columns], sources[1]).astype(BF16),
            dot_tn(sources[2][:, columns], sources[3]).astype(BF16),
        )

    def give_back(pre_grads):
        return call(
            lambda *refs: return_kernel(min(256, width), *refs),
            shape(padded, width),
            [VMEM] * 4,
            (pre_grads, w_gate[0], w_up[0], take_turned),
            16, 4 * slot_count * width * hidden_width, 4 * width * hidden_width,
        )

    def collect(came_back):
        return call(
            gather_kernel,
            shape(tok_dev, width),
            [VMEM, VMEM],
            (select_turned, came_back),
            12, 2 * padded * tok_dev * width, 4 * padded * width,
        )

    if chips > 1:
        farthest = chips // 2
        far = parts_of(slice(farthest * block, (farthest + 1) * block))
        sums = Sums(far, block, chips)
        sums.parts = parts_of(slice(None), sums.operands)
        returning = give_back(pre_grads)
        returned = None
        while sums.distance > 1:
            operands = sums.step()
            if returned is None:
                returning, _ = lax.optimization_barrier((returning, operands))
                returned = exchange(returning)
            sums.send(operands)
            latest = operands
        if returned is None:
            returned, latest = exchange(returning), returning
        returned, _ = lax.optimization_barrier((returned, latest))
        token_grads = collect(returned)
        weight_shapes = (
            shape(1, block, hidden_width),
            shape(1, block, hidden_width),
            shape(1, hidden_width, block),
        )
        weight_grads = sums.finish(weight_shapes, token_grads)
    else:
        token_grads = collect(exchange(give_back(pre_grads)))
        pre_part, down_part = parts_of(slice(None))
        weight_grads = (*(half[None] for half in jnp.split(pre_part, 2, axis=1)), down_part.T[None])
    return (token_grads, slot_grads.reshape(1, 1, slot_count), *weight_grads)


def solution(mesh):
    return jax.shard_map(
        body,
        mesh=mesh,
        in_specs=(
            P(("dp", "expert"), None),
            P(("dp", "expert"), None),
            P("dp", None, None),
            P("dp", "expert", None),
            P("expert", None, None),
            P("expert", None, None),
            P("expert", None, None),
        ),
        out_specs=(
            P(("dp", "expert"), None),
            P("dp", "expert", None),
            P("expert", "dp", None),
            P("expert", "dp", None),
            P("expert", None, "dp"),
        ),
        check_vma=False,
    )
```
